256 devices in a mesh: section: 4 (over x_hi, core), seq: 64 (over y, x_lo, z).
Axes of the slice: x: 4 (x_hi: 2, x_lo: 2; x = x_hi * 2 + x_lo), y: 4, z: 8, core: 2. Of those that a mesh axis runs over, the one named last changes fastest.
Arguments:
- layer_input: bfloat16 [4, 4096, 4, 1536], P('section', 'seq'), may hold values from -300 to 300
- norm_gain: float32 [4, 1536], P('section'), may hold values from 0.1 to 1.9
- queries: bfloat16 [4, 4096, 4, 1024], P('section', 'seq'), may hold values from -6 to 6
- key_states: bfloat16 [4, 4096, 4, 1024], P('section', 'seq'), may hold values from -6 to 6
- value_states: bfloat16 [4, 4096, 4, 1024], P('section', 'seq'), may hold values from -6 to 6
- out_grad: bfloat16 [4, 4096, 4, 1536], P('section', 'seq'), may hold values from -6 to 6
- out_weight: bfloat16 [4, 1024, 1536], P('section', 'seq'), may hold values from -0.1875 to 0.1875
- qkv_weight: bfloat16 [4, 1536, 3072], P('section', 'seq'), may hold values from -0.15625 to 0.15625
- lengths: int32 [4, 4], P('section'), may hold values from 2048 to 4096
Outputs:
- passed_grad: bfloat16 [4, 4096, 4, 1536], P('section', 'seq')
The draws below stay inside these ranges and needn't reach their ends.
All inputs are finite; a program needn't handle non-finite values.
Results may differ from the reference program's by a relative error of at most 0.0034.
Values may be sent and summed in bfloat16 or wider, within the bound.
No kernel may reach another device: no remote copies, remote signals or barrier semaphores. Data moves between devices by JAX's collectives and lax.ppermute only.
A program may use at most 128 MiB of HBM per device.

```python
import jax
import jax.numpy as jnp
from jax import lax

D = 1536
HEADS = 16
HS = 64
SEQS = 4
SECTIONS = 4
L = 4096


def draw_queries(key, part):
    values = jnp.clip(1.5 * jax.random.normal(jax.random.fold_in(key, 21), (SECTIONS, L, SEQS, HEADS * HS), jnp.float32), -6.0, 6.0)
    return values.astype(jnp.bfloat16)


def draw_key_states(key, part):
    values = jnp.clip(1.5 * jax.random.normal(jax.random.fold_in(key, 22), (SECTIONS, L, SEQS, HEADS * HS), jnp.float32), -6.0, 6.0)
    return values.astype(jnp.bfloat16)


def draw_layer_input(key, part):
    values = jnp.clip(jax.random.normal(jax.random.fold_in(key, 31), (SECTIONS, L, SEQS, D), jnp.float32), -6.0, 6.0)
    return values.astype(jnp.bfloat16)


def with_ends(values, stream_key, least, high):
    spot = [jax.random.randint(jax.random.fold_in(stream_key, axis), (), 0, length) for axis, length in enumerate(values.shape)]
    widest = values.shape.index(max(values.shape))
    next_to = spot[:widest] + [(spot[widest] + 1) % values.shape[widest]] + spot[widest + 1:]
    return values.at[tuple(spot)].set(least).at[tuple(next_to)].set(high)


def steps_of(stream_key, extent, cuts, least, high):
    level = 1.0
    for axis_at, blocks in cuts:
        draws = jax.random.uniform(jax.random.fold_in(jax.random.fold_in(stream_key, 6), axis_at), (blocks,), jnp.float32, least / len(cuts), high / len(cuts))
        level = level * jnp.repeat(jnp.exp(draws), extent[axis_at] // blocks).reshape((-1,) + (1,) * (len(extent) - 1 - axis_at))
    return level


def gaussian(rng, extent, scale, bound, shards=(), held_as=jnp.bfloat16):
    entries = jax.random.normal(rng, extent, jnp.float32) * scale
    if len(shards) > 0:
        entries = steps_of(rng, extent, shards, -0.22, 0.18) * entries
    return jnp.clip(entries, min=-bound, max=bound).astype(held_as)


def setup_inputs(seed: int = 0) -> dict:
    splits = jax.random.split(jax.random.key(seed), 10)
    return {
        "layer_input": draw_layer_input(jax.random.fold_in(splits[9], 71), 0),
        "norm_gain": jnp.clip(1.0 + 0.18 * jax.random.normal(splits[1], (SECTIONS, D), jnp.float32), 0.1, 1.9),
        "queries": draw_queries(jax.random.fold_in(splits[9], 71), 0),
        "key_states": draw_key_states(jax.random.fold_in(splits[9], 71), 0),
        "value_states": gaussian(splits[4], (SECTIONS, L, SEQS, HEADS * HS), 1.0, 6.0, ((0, 4), (1, 64))),
        "out_grad": gaussian(splits[5], (SECTIONS, L, SEQS, D), 1.0, 6.0, ((0, 4), (1, 64))),
        "out_weight": gaussian(splits[6], (SECTIONS, HEADS * HS, D), (HEADS * HS) ** -0.5, 0.1875, ((0, 4), (1, 64))),
        "qkv_weight": gaussian(splits[7], (SECTIONS, D, 3 * HEADS * HS), D ** -0.5, 0.15625, ((0, 4), (1, 64))),
        "lengths": with_ends(jax.random.randint(splits[8], (SECTIONS, SEQS), L // 2, L + 1), jax.random.fold_in(splits[8], 1), L // 2, L).astype(jnp.int32),
    }


EPSILON = 1e-05
MASKED = -1e+30

def item_backward(query_rows, key_rows, value_rows, grad_rows, key_valid):
    length = query_rows.shape[0]
    block = min(512, length)
    scale = HS ** (-0.5)
    offsets = jnp.arange(0, length, block).astype(jnp.int32)
    zeros = jnp.zeros((length, query_rows.shape[1]), jnp.float32)

    def step(carry, offset):
        key_total, value_total = carry
        query_block = lax.dynamic_slice_in_dim(query_rows, offset, block, 0)
        grad_block = lax.dynamic_slice_in_dim(grad_rows, offset, block, 0)
        scores = jnp.dot(query_block, key_rows.T, preferred_element_type=jnp.float32) * scale
        scores = jnp.where(key_valid[None, :], scores, MASKED)
        largest = lax.optimization_barrier(jnp.max(scores, axis=1, keepdims=True))
        weights = jnp.exp(scores - largest)
        probs = weights / lax.optimization_barrier(jnp.sum(weights, axis=1, keepdims=True))
        probs_low = probs.astype(jnp.bfloat16)
        grad_probs = jnp.dot(grad_block, value_rows.T, preferred_element_type=jnp.float32)
        centre = lax.optimization_barrier(jnp.sum(probs * grad_probs, axis=1, keepdims=True))
        grad_scores = (probs * (grad_probs - centre) * scale).astype(jnp.bfloat16)
        query_grad = jnp.dot(grad_scores, key_rows, preferred_element_type=jnp.float32)
        key_total = key_total + jnp.dot(grad_scores.T, query_block, preferred_element_type=jnp.float32)
        value_total = value_total + jnp.dot(probs_low.T, grad_block, preferred_element_type=jnp.float32)
        return ((key_total, value_total), query_grad.astype(jnp.bfloat16))
    (key_total, value_total), query_parts = lax.scan(step, (zeros, zeros), offsets)
    query_grad = query_parts.reshape(length, query_rows.shape[1])
    return (query_grad, key_total.astype(jnp.bfloat16), value_total.astype(jnp.bfloat16))

def to_items(array):
    return array.reshape(L, SEQS, HEADS, HS).transpose(1, 2, 0, 3).reshape(SEQS * HEADS, L, HS)

def from_items(array):
    return array.reshape(SEQS, HEADS, L, HS).transpose(2, 0, 1, 3).reshape(L * SEQS, HEADS * HS)

def section_backward(operands):
    layer_input, norm_gain, queries, key_states, value_states, out_grad, out_weight, qkv_weight, lengths = operands
    flat_grad = out_grad.reshape(L * SEQS, D)
    attn_grad = jnp.dot(flat_grad, out_weight.T, preferred_element_type=jnp.float32).astype(jnp.bfloat16)
    attn_grad = attn_grad.reshape(L, SEQS, HEADS * HS)
    positions = jnp.arange(L).astype(jnp.int32)
    valid = positions[None, :] < lengths[:, None]
    valid_items = jnp.repeat(valid, HEADS, axis=0)
    query_grad, key_gradient, value_grad = lax.map(lambda group: item_backward(*group), (to_items(queries), to_items(key_states), to_items(value_states), to_items(attn_grad), valid_items))
    joined = jnp.concatenate([from_items(query_grad), from_items(key_gradient), from_items(value_grad)], axis=1)
    norm_grad = jnp.dot(joined, qkv_weight.T, preferred_element_type=jnp.float32)
    inputs = layer_input.reshape(L * SEQS, D).astype(jnp.float32)
    row_average = lax.optimization_barrier(jnp.mean(inputs, axis=1, keepdims=True))
    centered_input = inputs - row_average
    var = lax.optimization_barrier(jnp.mean(centered_input * centered_input, axis=1, keepdims=True))
    inverse_deviation = 1.0 / jnp.sqrt(var + EPSILON)
    normalized_input = centered_input * inverse_deviation
    scaled_rows = norm_grad * norm_gain[None, :]
    residual_branch = inverse_deviation * (scaled_rows - lax.optimization_barrier(jnp.mean(scaled_rows, axis=1, keepdims=True)) - normalized_input * lax.optimization_barrier(jnp.mean(scaled_rows * normalized_input, axis=1, keepdims=True)))
    input_grad = (flat_grad.astype(jnp.float32) + residual_branch).astype(jnp.bfloat16)
    return input_grad.reshape(L, SEQS, D)

def reference(layer_input, norm_gain, queries, key_states, value_states, out_grad, out_weight, qkv_weight, lengths):
    input_grad = lax.map(section_backward, (layer_input, norm_gain, queries, key_states, value_states, out_grad, out_weight, qkv_weight, lengths))
    return jnp.roll(input_grad, -1, axis=0)
```

```python
import functools

import jax
import jax.numpy as jnp
from jax import lax
from jax.experimental import pallas as pl
from jax.experimental.pallas import tpu as pltpu
from jax.sharding import PartitionSpec as P

HEADS = 16
HS = 64
EPSILON = 1e-05
MASKED = -1e30
SCALE = HS**-0.5
ROW_DOT = (((1,), (1,)), ((), ()))
PLAIN_DOT = (((1,), (0,)), ((), ()))
MIB = 1024 * 1024
QB = 256
KB = 256
Y, X, Z = 4, 2, 8
BF16 = jnp.bfloat16
F32 = jnp.float32
WHOLE = pl.BlockSpec(memory_space=pltpu.VMEM)


def cost(flops, moved, exps=0):
    return pl.CostEstimate(flops=flops, bytes_accessed=moved, transcendentals=exps)


def halves(even, odd):
    first = jnp.concatenate([even[:, :HS], odd[:, :HS]], axis=1)
    second = jnp.concatenate([even[:, HS:], odd[:, HS:]], axis=1)
    return first, second


def seq_pairs(dy, dx, dz):
    pairs = []
    for y in range(Y):
        for x in range(X):
            for z in range(Z):
                to = ((y + dy) % Y) * X * Z + ((x + dx) % X) * Z + (z + dz) % Z
                pairs.append((y * X * Z + x * Z + z, to))
    return pairs


def pack_kernel(q_ref, k_ref, v_ref, out_ref):
    half = q_ref.shape[0] // 2
    for n, ref in enumerate((q_ref, k_ref, v_ref)):
        for pair in range(ref.shape[1] // 128):
            tile = ref[:, pair * 128 : (pair + 1) * 128]
            first, second = halves(tile[:half], tile[half:])
            out_ref[2 * pair, n * half : (n + 1) * half, :] = first
            out_ref[2 * pair + 1, n * half : (n + 1) * half, :] = second


def pack_items(q, k, v):
    frames, lanes = q.shape
    out = jax.ShapeDtypeStruct((lanes // HS, 3 * frames // 2, 128), BF16)
    return pl.pallas_call(
        pack_kernel,
        out_shape=out,
        in_specs=[WHOLE] * 3,
        out_specs=WHOLE,
        compiler_params=pltpu.CompilerParams(vmem_limit_bytes=16 * MIB),
        cost_estimate=cost(0, 3 * MIB),
    )(q, k, v)


def place_kernel(owner_ref, *refs):
    out_ref = refs[-1]
    for n, ref in enumerate(refs[:-1]):
        out_ref[owner_ref[n]] = ref[...]


def place(owners, pieces):
    out = jax.ShapeDtypeStruct((len(pieces),) + pieces[0].shape, BF16)
    size = 2 * len(pieces) * pieces[0].size
    return pl.pallas_call(
        place_kernel,
        out_shape=out,
        in_specs=[pl.BlockSpec(memory_space=pltpu.SMEM)] + [WHOLE] * len(pieces),
        out_specs=WHOLE,
        compiler_params=pltpu.CompilerParams(vmem_limit_bytes=2 * size + 4 * MIB),
        cost_estimate=cost(0, 2 * size),
    )(owners, *pieces)


def project_kernel(owner_ref, grad_ref, *refs):
    out_ref = refs[-1]
    records = grad_ref.shape[0] // 64
    grads = grad_ref[...]
    for n, ref in enumerate(refs[:-1]):
        owner = owner_ref[n]
        tile = lax.dot_general(grads, ref[...], ROW_DOT, preferred_element_type=F32).astype(BF16)
        for r in range(records):
            first, second = halves(tile[r * 64 : r * 64 + 32], tile[r * 64 + 32 : r * 64 + 64])
            out_ref[r * HEADS + 2 * owner] = first
            out_ref[r * HEADS + 2 * owner + 1] = second


def project(owners, grads, pieces):
    rows, width = grads.shape
    items = (rows // 64) * HEADS
    return pl.pallas_call(
        project_kernel,
        out_shape=jax.ShapeDtypeStruct((items, 32, 128), BF16),
        in_specs=[pl.BlockSpec(memory_space=pltpu.SMEM)] + [WHOLE] * (1 + len(pieces)),
        out_specs=WHOLE,
        compiler_params=pltpu.CompilerParams(vmem_limit_bytes=20 * MIB),
        cost_estimate=cost(2 * rows * width * 1024, 2 * (rows * width + 1024 * width + rows * 1024)),
    )(owners, grads, *pieces)


def fold(values, op):
    return op(values.reshape(values.shape[0] // 8, 8, values.shape[1]), axis=0)


def weights_kernel(length_ref, r_ref, w_ref, l_ref, qt_ref, kt_ref, kz_ref, s_ref):
    step = pl.program_id(0)
    sources = r_ref.shape[0]
    rows = sources * 32
    length = 2 * rows

    @pl.when(step == 0)
    def _():
        valid = length_ref[0]
        packed_q = r_ref[:, 0:32, :].reshape(rows, 128)
        packed_k = r_ref[:, 32:64, :].reshape(rows, 128)
        q_turned = packed_q.T
        k_turned = packed_k.T
        for half in range(2):
            qt_ref[0:HS, half * rows : (half + 1) * rows] = q_turned[half * HS : (half + 1) * HS, :]
            kt_ref[:, half * rows : (half + 1) * rows] = k_turned[half * HS : (half + 1) * HS, :]
        row_id = lax.broadcasted_iota(jnp.int32, (HS, length), 0)
        qt_ref[HS:128, :] = jnp.where(row_id == 0, 1.0, 0.0).astype(BF16)
        spot = lax.broadcasted_iota(jnp.int32, (rows, HS), 0)
        lane = lax.broadcasted_iota(jnp.int32, (rows, HS), 1)
        for half in range(2):
            frame = (spot // 32) * 64 + half * 32 + spot % 32
            bias = jnp.where((lane == 0) & (frame >= valid), MASKED, 0.0).astype(BF16)
            keys = packed_k[:, half * HS : (half + 1) * HS] * SCALE
            kz_ref[half * rows : (half + 1) * rows, :] = jnp.concatenate([keys.astype(BF16), bias], axis=1)

    queries = qt_ref[:, pl.ds(pl.multiple_of(step * QB, QB), QB)]

    def first(j, top):
        at = pl.ds(pl.multiple_of(j * KB, KB), KB)
        s = lax.dot_general(kz_ref[at, :], queries, PLAIN_DOT, preferred_element_type=F32)
        s_ref[at, :] = s
        return jnp.maximum(top, fold(s, jnp.max))

    top = lax.fori_loop(0, length // KB, first, jnp.full((8, QB), -jnp.inf, F32), unroll=2)
    top = jnp.max(top, axis=0, keepdims=True)

    def second(j, total):
        at = pl.ds(pl.multiple_of(j * KB, KB), KB)
        w = jnp.exp(s_ref[at, :] - top)
        w_ref[0, at, :] = w.astype(BF16)
        return total + fold(w, jnp.sum)

    total = lax.fori_loop(0, length // KB, second, jnp.zeros((8, QB), F32), unroll=2)
    l_ref[...] = jnp.sum(total, axis=0, keepdims=True)


def softmax_weights(valid, received):
    length = received.shape[0] * 64
    blocks = length // QB
    fixed = lambda shape: pl.BlockSpec(shape, lambda i: (0,) * len(shape))
    return pl.pallas_call(
        weights_kernel,
        grid=(blocks,),
        out_shape=[
            jax.ShapeDtypeStruct((blocks, length, QB), BF16),
            jax.ShapeDtypeStruct((1, length), F32),
            jax.ShapeDtypeStruct((128, length), BF16),
            jax.ShapeDtypeStruct((HS, length), BF16),
        ],
        in_specs=[pl.BlockSpec(memory_space=pltpu.SMEM), WHOLE],
        out_specs=[
            pl.BlockSpec((1, length, QB), lambda i: (i, 0, 0)),
            pl.BlockSpec((1, QB), lambda i: (0, i)),
            fixed((128, length)),
            fixed((HS, length)),
        ],
        scratch_shapes=[pltpu.VMEM((length, 128), BF16), pltpu.VMEM((length, QB), F32)],
        compiler_params=pltpu.CompilerParams(vmem_limit_bytes=40 * MIB),
        cost_estimate=cost(8 * length * length * HS, 2 * length * length, length * length),
    )(valid, received)


def grads_kernel(w_ref, l_ref, qt_ref, kt_ref, r_ref, g_ref, dq_ref, dkv_ref, gt_ref, dp_ref, acc_ref, dqt_ref):
    step = pl.program_id(0)
    sources = r_ref.shape[0]
    rows = sources * 32
    length = 2 * rows
    per = KB // 32

    @pl.when(step == 0)
    def _():
        turned = g_ref[...].reshape(rows, 128).T
        for half in range(2):
            gt_ref[:, half * rows : (half + 1) * rows] = turned[half * HS : (half + 1) * HS, :]
        acc_ref[...] = jnp.zeros_like(acc_ref)

    here = pl.ds(pl.multiple_of(step * QB, QB), QB)
    grads = gt_ref[:, here]
    none = jnp.zeros((HS, QB), BF16)
    inverse = 1.0 / l_ref[:, here]

    def first(half, side, j, centre):
        at = pl.ds(pl.multiple_of(half * rows + j * KB, KB), KB)
        values = r_ref[pl.ds(j * per, per), 64:96, :].reshape(KB, 128)
        dp = lax.dot_general(values, side, PLAIN_DOT, preferred_element_type=F32)
        dp_ref[at, :] = dp
        return centre + fold(w_ref[0, at, :].astype(F32) * dp, jnp.sum)

    centre = jnp.zeros((8, QB), F32)
    for half in range(2):
        side = jnp.concatenate([grads, none] if half == 0 else [none, grads], axis=0)
        centre = lax.fori_loop(0, rows // KB, functools.partial(first, half, side), centre, unroll=2)
    centre = jnp.sum(centre, axis=0, keepdims=True) * inverse

    scaled_q = (qt_ref[0:HS, here].astype(F32) * (inverse * SCALE)).astype(BF16)
    scaled_g = (grads.astype(F32) * inverse).astype(BF16)
    side_t = jnp.concatenate([scaled_q, none], axis=0)
    side_w = jnp.concatenate([none, scaled_g], axis=0)

    def second(j, dqt):
        at = pl.ds(pl.multiple_of(j * KB, KB), KB)
        w = w_ref[0, at, :]
        t = (w.astype(F32) * (dp_ref[at, :] - centre)).astype(BF16)
        acc_ref[at, :] += lax.dot_general(
            t, side_t, ROW_DOT, preferred_element_type=F32
        ) + lax.dot_general(w, side_w, ROW_DOT, preferred_element_type=F32)
        return dqt + lax.dot_general(kt_ref[:, at], t, PLAIN_DOT, preferred_element_type=F32)

    dqt = lax.fori_loop(0, length // KB, second, jnp.zeros((HS, QB), F32), unroll=2)
    dqt = dqt * (inverse * SCALE)
    steps = rows // QB

    @pl.when(step < steps)
    def _():
        dqt_ref[0:HS, pl.ds(pl.multiple_of(step * QB, QB), QB)] = dqt

    @pl.when(step >= steps)
    def _():
        dqt_ref[HS:128, pl.ds(pl.multiple_of((step - steps) * QB, QB), QB)] = dqt

    @pl.when(step == 2 * steps - 1)
    def _():
        dq_ref[...] = dqt_ref[...].T.astype(BF16).reshape(sources, 32, 128)
        for half in range(2):
            part = acc_ref[half * rows : (half + 1) * rows, :].astype(BF16)
            dkv_ref[:, half * 32 : (half + 1) * 32, :] = part.reshape(sources, 32, 128)


def attention_grads(weights, sums, queries_t, keys_t, received, received_grads):
    blocks, length, _ = weights.shape
    sources = received.shape[0]
    return pl.pallas_call(
        grads_kernel,
        grid=(blocks,),
        out_shape=[
            jax.ShapeDtypeStruct((sources, 32, 128), BF16),
            jax.ShapeDtypeStruct((sources, 64, 128), BF16),
        ],
        in_specs=[pl.BlockSpec((1, length, QB), lambda i: (i, 0, 0))] + [WHOLE] * 5,
        out_specs=[WHOLE, WHOLE],
        scratch_shapes=[
            pltpu.VMEM((HS, length), BF16),
            pltpu.VMEM((length, QB), F32),
            pltpu.VMEM((length, 128), F32),
            pltpu.VMEM((128, length // 2), F32),
        ],
        compiler_params=pltpu.CompilerParams(vmem_limit_bytes=40 * MIB),
        cost_estimate=cost(32 * length * length * HS, 2 * length * length),
    )(weights, sums, queries_t, keys_t, received, received_grads)


def finish_kernel(dq_ref, dkv_ref, w_ref, x_ref, g_ref, gain_ref, out_ref, j_ref, n_ref):
    records = x_ref.shape[0]
    frames = x_ref.shape[1]
    width = x_ref.shape[2]
    features = HEADS * HS
    for r in range(records):
        for pair in range(HEADS // 2):
            item = r * HEADS + 2 * pair
            at = slice(pair * 128, (pair + 1) * 128)
            first, second = halves(dq_ref[item], dq_ref[item + 1])
            j_ref[r * frames : r * frames + 32, at] = first
            j_ref[r * frames + 32 : (r + 1) * frames, at] = second
            keys, values = halves(dkv_ref[item], dkv_ref[item + 1])
            span = slice(r * frames, (r + 1) * frames)
            j_ref[span, features + pair * 128 : features + (pair + 1) * 128] = keys
            j_ref[span, 2 * features + pair * 128 : 2 * features + (pair + 1) * 128] = values
    step = 256
    for n in range(width // step):
        n_ref[:, n * step : (n + 1) * step] = lax.dot_general(
            j_ref[...], w_ref[n * step : (n + 1) * step, :], ROW_DOT, preferred_element_type=F32
        )
    for r in range(records):
        x = x_ref[r].astype(F32)
        centred = x - jnp.mean(x, axis=1, keepdims=True)
        var = jnp.mean(centred * centred, axis=1, keepdims=True)
        deviation = lax.rsqrt(var + EPSILON)
        normal = centred * deviation
        scaled = n_ref[r * frames : (r + 1) * frames, :] * gain_ref[...]
        residual = deviation * (
            scaled
            - jnp.mean(scaled, axis=1, keepdims=True)
            - normal * jnp.mean(scaled * normal, axis=1, keepdims=True)
        )
        out_ref[r] = (g_ref[r].astype(F32) + residual).astype(BF16)


def finish(dq, dkv, weight, inputs, grads, gain):
    records, frames, width = inputs.shape
    return pl.pallas_call(
        finish_kernel,
        out_shape=jax.ShapeDtypeStruct(inputs.shape, BF16),
        in_specs=[WHOLE] * 6,
        out_specs=WHOLE,
        scratch_shapes=[
            pltpu.VMEM((records * frames, 3 * HEADS * HS), BF16),
            pltpu.VMEM((records * frames, width), F32),
        ],
        compiler_params=pltpu.CompilerParams(vmem_limit_bytes=40 * MIB),
        cost_estimate=cost(2 * records * frames * width * 3072, 2 * 3072 * width),
    )(dq, dkv, weight, inputs, grads, gain)


def exchange(items):
    return lax.all_to_all(items, "seq", split_axis=0, concat_axis=0, tiled=True)


def gathered_pieces(rows, seq):
    z = lax.rem(seq, Z)
    others = [lax.ppermute(rows, "seq", seq_pairs(0, 0, k)) for k in range(1, Z)]
    owners = jnp.stack([lax.rem(z - k + Z, Z) for k in range(Z)])
    group = place(owners, [rows] + others).reshape(Z * rows.shape[0], rows.shape[1])
    pieces = [group]
    steps = [(0, 0)]
    for dy, dx in ((0, 1), (1, 0), (3, 0), (1, 1), (3, 1), (2, 0), (2, 1)):
        pieces.append(lax.ppermute(group, "seq", seq_pairs(dy, dx, 0)))
        steps.append((dy, dx))
    y = seq // (X * Z)
    x = lax.rem(seq // Z, X)
    places = jnp.stack([lax.rem(y - dy + Y, Y) * X + lax.rem(x - dx + X, X) for dy, dx in steps])
    return places, pieces


def on_device(
    layer_input,
    norm_gain,
    queries,
    key_states,
    value_states,
    out_grad,
    out_weight,
    qkv_weight,
    lengths,
):
    frames, records, features = queries.shape[1:]
    width = out_grad.shape[3]
    seq = lax.axis_index("seq").astype(jnp.int32)
    flat = lambda array: array[0].reshape(frames, records * features)
    packed = pack_items(flat(queries), flat(key_states), flat(value_states))
    received = exchange(packed)
    grads = out_grad[0].transpose(1, 0, 2)
    inputs = layer_input[0].transpose(1, 0, 2)
    pairs, out_pieces = gathered_pieces(out_weight[0], seq)
    attn_grad = project(pairs, grads.reshape(records * frames, width), out_pieces)
    received_grads = exchange(attn_grad)
    record = seq // HEADS
    valid = jnp.sum(jnp.where(jnp.arange(records) == record, lengths[0], 0)).reshape(1)
    weights, sums, queries_t, keys_t = softmax_weights(valid, received)
    dq, dkv = attention_grads(weights, sums, queries_t, keys_t, received, received_grads)
    dq = exchange(dq)
    dkv = exchange(dkv)
    places, qkv_pieces = gathered_pieces(qkv_weight[0], seq)
    weight = place(places, qkv_pieces).reshape(width, 3 * features)
    result = finish(dq, dkv, weight, inputs, grads, norm_gain)
    count = lax.axis_size("section")
    moved = lax.ppermute(result, "section", [(i, (i - 1) % count) for i in range(count)])
    return moved.transpose(1, 0, 2)[None]


def solution(mesh):
    rows = P("section", "seq", None, None)
    in_specs = (
        rows,
        P("section", None),
        rows,
        rows,
        rows,
        rows,
        P("section", "seq", None),
        P("section", "seq", None),
        P("section", None),
    )
    return jax.shard_map(on_device, mesh=mesh, in_specs=in_specs, out_specs=rows, check_vma=False)
```

```python
import functools

import jax
import jax.numpy as jnp
from jax import lax
from jax.experimental import pallas as pl
from jax.experimental.pallas import tpu as pltpu
from jax.sharding import PartitionSpec as P

HEADS = 16
HS = 64
EPSILON = 1e-05
MASKED = -1e30
SCALE = HS**-0.5
ROW_DOT = (((1,), (1,)), ((), ()))
PLAIN_DOT = (((1,), (0,)), ((), ()))
MIB = 1024 * 1024
QB = 256
KB = 256
UNROLL1 = True
UNROLL2 = True
Y, X, Z = 4, 2, 8
BF16 = jnp.bfloat16
F32 = jnp.float32
WHOLE = pl.BlockSpec(memory_space=pltpu.VMEM)


def cost(flops, moved, exps=0):
    return pl.CostEstimate(flops=flops, bytes_accessed=moved, transcendentals=exps)


def halves(even, odd):
    first = jnp.concatenate([even[:, :HS], odd[:, :HS]], axis=1)
    second = jnp.concatenate([even[:, HS:], odd[:, HS:]], axis=1)
    return first, second


def seq_pairs(dy, dx, dz):
    pairs = []
    for y in range(Y):
        for x in range(X):
            for z in range(Z):
                to = ((y + dy) % Y) * X * Z + ((x + dx) % X) * Z + (z + dz) % Z
                pairs.append((y * X * Z + x * Z + z, to))
    return pairs


def pack_kernel(q_ref, k_ref, v_ref, out_ref):
    half = q_ref.shape[0] // 2
    for n, ref in enumerate((q_ref, k_ref, v_ref)):
        for pair in range(ref.shape[1] // 128):
            tile = ref[:, pair * 128 : (pair + 1) * 128]
            first, second = halves(tile[:half], tile[half:])
            out_ref[2 * pair, n * half : (n + 1) * half, :] = first
            out_ref[2 * pair + 1, n * half : (n + 1) * half, :] = second


def pack_items(q, k, v):
    frames, lanes = q.shape
    out = jax.ShapeDtypeStruct((lanes // HS, 3 * frames // 2, 128), BF16)
    return pl.pallas_call(
        pack_kernel,
        out_shape=out,
        in_specs=[WHOLE] * 3,
        out_specs=WHOLE,
        compiler_params=pltpu.CompilerParams(vmem_limit_bytes=16 * MIB),
        cost_estimate=cost(0, 3 * MIB),
    )(q, k, v)


def place_kernel(owner_ref, *refs):
    out_ref = refs[-1]
    for n, ref in enumerate(refs[:-1]):
        out_ref[owner_ref[n]] = ref[...]


def place(owners, pieces):
    out = jax.ShapeDtypeStruct((len(pieces),) + pieces[0].shape, BF16)
    size = 2 * len(pieces) * pieces[0].size
    return pl.pallas_call(
        place_kernel,
        out_shape=out,
        in_specs=[pl.BlockSpec(memory_space=pltpu.SMEM)] + [WHOLE] * len(pieces),
        out_specs=WHOLE,
        compiler_params=pltpu.CompilerParams(vmem_limit_bytes=2 * size + 4 * MIB),
        cost_estimate=cost(0, 2 * size),
    )(owners, *pieces)


def project_kernel(owner_ref, grad_ref, *refs):
    out_ref = refs[-1]
    records = grad_ref.shape[0] // 64
    grads = grad_ref[...]
    for n, ref in enumerate(refs[:-1]):
        owner = owner_ref[n]
        tile = lax.dot_general(grads, ref[...], ROW_DOT, preferred_element_type=F32).astype(BF16)
        for r in range(records):
            first, second = halves(tile[r * 64 : r * 64 + 32], tile[r * 64 + 32 : r * 64 + 64])
            out_ref[r * HEADS + 2 * owner] = first
            out_ref[r * HEADS + 2 * owner + 1] = second


def project(owners, grads, pieces):
    rows, width = grads.shape
    items = (rows // 64) * HEADS
    return pl.pallas_call(
        project_kernel,
        out_shape=jax.ShapeDtypeStruct((items, 32, 128), BF16),
        in_specs=[pl.BlockSpec(memory_space=pltpu.SMEM)] + [WHOLE] * (1 + len(pieces)),
        out_specs=WHOLE,
        compiler_params=pltpu.CompilerParams(vmem_limit_bytes=20 * MIB),
        cost_estimate=cost(2 * rows * width * 1024, 2 * (rows * width + 1024 * width + rows * 1024)),
    )(owners, grads, *pieces)


def fold(values, op):
    return op(values.reshape(values.shape[0] // 8, 8, values.shape[1]), axis=0)


def prepare_kernel(length_ref, r_ref, kz_ref, qt_ref, kt_ref):
    sources = r_ref.shape[0]
    rows = sources * 32
    length = 2 * rows
    valid = length_ref[0]
    packed_q = r_ref[:, 0:32, :].reshape(rows, 128)
    packed_k = r_ref[:, 32:64, :].reshape(rows, 128)
    q_turned = packed_q.T
    k_turned = packed_k.T
    for half in range(2):
        qt_ref[0:HS, half * rows : (half + 1) * rows] = q_turned[half * HS : (half + 1) * HS, :]
        kt_ref[:, half * rows : (half + 1) * rows] = k_turned[half * HS : (half + 1) * HS, :]
    row_id = lax.broadcasted_iota(jnp.int32, (HS, length), 0)
    qt_ref[HS:128, :] = jnp.where(row_id == 0, 1.0, 0.0).astype(BF16)
    spot = lax.broadcasted_iota(jnp.int32, (rows, HS), 0)
    lane = lax.broadcasted_iota(jnp.int32, (rows, HS), 1)
    for half in range(2):
        frame = (spot // 32) * 64 + half * 32 + spot % 32
        bias = jnp.where((lane == 0) & (frame >= valid), MASKED, 0.0).astype(BF16)
        keys = packed_k[:, half * HS : (half + 1) * HS] * SCALE
        kz_ref[half * rows : (half + 1) * rows, :] = jnp.concatenate([keys.astype(BF16), bias], axis=1)


def prepare(valid, received):
    length = received.shape[0] * 64
    return pl.pallas_call(
        prepare_kernel,
        out_shape=[
            jax.ShapeDtypeStruct((length, 128), BF16),
            jax.ShapeDtypeStruct((128, length), BF16),
            jax.ShapeDtypeStruct((HS, length), BF16),
        ],
        in_specs=[pl.BlockSpec(memory_space=pltpu.SMEM), WHOLE],
        out_specs=[WHOLE] * 3,
        compiler_params=pltpu.CompilerParams(vmem_limit_bytes=16 * MIB),
        cost_estimate=cost(0, 4 * MIB),
    )(valid, received)


def weights_kernel(kz_ref, qt_ref, w_ref, l_ref, s_ref):
    length = kz_ref.shape[0]
    queries = qt_ref[...]

    def first(j, top):
        at = pl.ds(pl.multiple_of(j * KB, KB), KB)
        s = lax.dot_general(kz_ref[at, :], queries, PLAIN_DOT, preferred_element_type=F32)
        s_ref[at, :] = s
        return jnp.maximum(top, fold(s, jnp.max))

    top = lax.fori_loop(0, length // KB, first, jnp.full((8, QB), -jnp.inf, F32), unroll=UNROLL1)
    top = jnp.max(top, axis=0, keepdims=True)

    def second(j, total):
        at = pl.ds(pl.multiple_of(j * KB, KB), KB)
        w = jnp.exp(s_ref[at, :] - top)
        w_ref[0, at, :] = w
        return total + fold(w, jnp.sum)

    total = lax.fori_loop(0, length // KB, second, jnp.zeros((8, QB), F32), unroll=UNROLL1)
    l_ref[...] = jnp.sum(total, axis=0, keepdims=True)


def softmax_weights(part, keys, queries_t):
    length = keys.shape[0]
    blocks = length // QB // 2
    return pl.pallas_call(
        weights_kernel,
        grid=(blocks,),
        out_shape=[
            jax.ShapeDtypeStruct((blocks, length, QB), F32),
            jax.ShapeDtypeStruct((1, length // 2), F32),
        ],
        in_specs=[WHOLE, pl.BlockSpec((128, QB), lambda i: (0, part * blocks + i))],
        out_specs=[
            pl.BlockSpec((1, length, QB), lambda i: (i, 0, 0)),
            pl.BlockSpec((1, QB), lambda i: (0, i)),
        ],
        scratch_shapes=[pltpu.VMEM((length, QB), F32)],
        compiler_params=pltpu.CompilerParams(vmem_limit_bytes=24 * MIB),
        cost_estimate=cost(4 * length * length * HS, 2 * length * length, length * length // 2),
    )(keys, queries_t)


def grads_kernel(part, w_ref, l_ref, qt_ref, kt_ref, r_ref, g_ref, *refs):
    if part == 0:
        dq_ref, acc_ref, gt_ref, dp_ref = refs
    else:
        begun_dq_ref, begun_ref, out_ref, gt_ref, dp_ref, acc_ref, dq_ref = refs
    step = pl.program_id(0)
    sources = r_ref.shape[0]
    rows = sources * 32
    length = 2 * rows
    per = KB // 32

    @pl.when(step == 0)
    def _():
        gt_ref[...] = g_ref[...].reshape(rows, 128).T[part * HS : (part + 1) * HS, :]
        acc_ref[...] = jnp.zeros_like(acc_ref) if part == 0 else begun_ref[...]

    here = pl.ds(pl.multiple_of(step * QB, QB), QB)
    grads = gt_ref[:, here]
    none = jnp.zeros((HS, QB), BF16)
    inverse = 1.0 / l_ref[...]

    def first(half, side, j, centre):
        at = pl.ds(pl.multiple_of(half * rows + j * KB, KB), KB)
        values = r_ref[pl.ds(j * per, per), 64:96, :].reshape(KB, 128)
        dp = lax.dot_general(values, side, PLAIN_DOT, preferred_element_type=F32)
        dp_ref[at, :] = dp
        return centre + fold(w_ref[0, at, :] * inverse * dp, jnp.sum)

    centre = jnp.zeros((8, QB), F32)
    for half in range(2):
        side = jnp.concatenate([grads, none] if half == 0 else [none, grads], axis=0)
        centre = lax.fori_loop(0, rows // KB, functools.partial(first, half, side), centre, unroll=UNROLL2)
    centre = jnp.sum(centre, axis=0, keepdims=True)

    scaled_q = (qt_ref[0:HS, :] * SCALE).astype(BF16)
    side_t = jnp.concatenate([scaled_q, none], axis=0)
    side_w = jnp.concatenate([none, grads], axis=0)

    def second(j, dqt):
        at = pl.ds(pl.multiple_of(j * KB, KB), KB)
        p = w_ref[0, at, :] * inverse
        t = (p * (dp_ref[at, :] - centre)).astype(BF16)
        acc_ref[at, :] += lax.dot_general(
            t, side_t, ROW_DOT, preferred_element_type=F32
        ) + lax.dot_general(p.astype(BF16), side_w, ROW_DOT, preferred_element_type=F32)
        return dqt + lax.dot_general(kt_ref[:, at], t, PLAIN_DOT, preferred_element_type=F32)

    dqt = lax.fori_loop(0, length // KB, second, jnp.zeros((HS, QB), F32), unroll=UNROLL2)
    dq_ref[:, here] = dqt * SCALE

    if part == 1:

        @pl.when(step == pl.num_programs(0) - 1)
        def _():
            both = jnp.concatenate([begun_dq_ref[...], dq_ref[...]], axis=0)
            out_ref[:, 0:32, :] = both.T.astype(BF16).reshape(sources, 32, 128)
            for half in range(2):
                lanes = acc_ref[half * rows : (half + 1) * rows, :].astype(BF16)
                at = slice(32 + half * 32, 64 + half * 32)
                out_ref[:, at, :] = lanes.reshape(sources, 32, 128)


def attention_grads(part, weights, sums, queries_t, keys_t, received, received_grads, begun=()):
    blocks, length, _ = weights.shape
    sources = received.shape[0]
    dq = jax.ShapeDtypeStruct((HS, length // 2), F32)
    acc = jax.ShapeDtypeStruct((length, 128), F32)
    scratch = [pltpu.VMEM((HS, length // 2), BF16), pltpu.VMEM((length, QB), F32)]
    if part == 0:
        out_shape = [dq, acc]
        out_specs = [WHOLE, WHOLE]
    else:
        out_shape = jax.ShapeDtypeStruct((sources, 96, 128), BF16)
        out_specs = WHOLE
        scratch += [pltpu.VMEM((length, 128), F32), pltpu.VMEM((HS, length // 2), F32)]
    return pl.pallas_call(
        functools.partial(grads_kernel, part),
        grid=(blocks,),
        out_shape=out_shape,
        in_specs=[
            pl.BlockSpec((1, length, QB), lambda i: (i, 0, 0)),
            pl.BlockSpec((1, QB), lambda i: (0, i)),
            pl.BlockSpec((128, QB), lambda i: (0, part * blocks + i)),
        ]
        + [WHOLE] * (3 + len(begun)),
        out_specs=out_specs,
        scratch_shapes=scratch,
        compiler_params=pltpu.CompilerParams(vmem_limit_bytes=40 * MIB),
        cost_estimate=cost(16 * length * length * HS, 2 * length * length),
    )(weights, sums, queries_t, keys_t, received, received_grads, *begun)


def finish_kernel(back_ref, w_ref, x_ref, g_ref, gain_ref, out_ref, j_ref, n_ref):
    records = x_ref.shape[0]
    frames = x_ref.shape[1]
    width = x_ref.shape[2]
    features = HEADS * HS
    for r in range(records):
        for pair in range(HEADS // 2):
            item = r * HEADS + 2 * pair
            at = slice(pair * 128, (pair + 1) * 128)
            first, second = halves(back_ref[item, 0:32], back_ref[item + 1, 0:32])
            j_ref[r * frames : r * frames + 32, at] = first
            j_ref[r * frames + 32 : (r + 1) * frames, at] = second
            keys, values = halves(back_ref[item, 32:96], back_ref[item + 1, 32:96])
            span = slice(r * frames, (r + 1) * frames)
            j_ref[span, features + pair * 128 : features + (pair + 1) * 128] = keys
            j_ref[span, 2 * features + pair * 128 : 2 * features + (pair + 1) * 128] = values
    step = 256
    for n in range(width // step):
        n_ref[:, n * step : (n + 1) * step] = lax.dot_general(
            j_ref[...], w_ref[n * step : (n + 1) * step, :], ROW_DOT, preferred_element_type=F32
        )
    for r in range(records):
        x = x_ref[r].astype(F32)
        centred = x - jnp.mean(x, axis=1, keepdims=True)
        var = jnp.mean(centred * centred, axis=1, keepdims=True)
        deviation = lax.rsqrt(var + EPSILON)
        normal = centred * deviation
        scaled = n_ref[r * frames : (r + 1) * frames, :] * gain_ref[...]
        residual = deviation * (
            scaled
            - jnp.mean(scaled, axis=1, keepdims=True)
            - normal * jnp.mean(scaled * normal, axis=1, keepdims=True)
        )
        out_ref[r] = (g_ref[r].astype(F32) + residual).astype(BF16)


def finish(back, weight, inputs, grads, gain):
    records, frames, width = inputs.shape
    return pl.pallas_call(
        finish_kernel,
        out_shape=jax.ShapeDtypeStruct(inputs.shape, BF16),
        in_specs=[WHOLE] * 5,
        out_specs=WHOLE,
        scratch_shapes=[
            pltpu.VMEM((records * frames, 3 * HEADS * HS), BF16),
            pltpu.VMEM((records * frames, width), F32),
        ],
        compiler_params=pltpu.CompilerParams(vmem_limit_bytes=40 * MIB),
        cost_estimate=cost(2 * records * frames * width * 3072, 2 * 3072 * width),
    )(back, weight, inputs, grads, gain)


def exchange(items, groups=None):
    return lax.all_to_all(items, "seq", split_axis=0, concat_axis=0, tiled=True, axis_index_groups=groups)


def after(value, *others):
    return lax.optimization_barrier((value,) + others)[0]


def across(rows, dy, dx):
    return lax.ppermute(rows, "seq", seq_pairs(dy, dx, 0))


NEAR = ((0, 1), (1, 0), (3, 0))
DIAGONAL = ((1, 1), (3, 1))
FAR = ((2, 0), (2, 1))
STEPS = ((0, 0),) + NEAR + DIAGONAL + FAR


def on_device(
    layer_input,
    norm_gain,
    queries,
    key_states,
    value_states,
    out_grad,
    out_weight,
    qkv_weight,
    lengths,
):
    frames, records, features = queries.shape[1:]
    width = out_grad.shape[3]
    seq = lax.axis_index("seq").astype(jnp.int32)
    y, x, z = seq // (X * Z), lax.rem(seq // Z, X), lax.rem(seq, Z)
    along_z = jnp.stack([lax.rem(z - k + Z, Z) for k in range(Z)])
    places = jnp.stack([lax.rem(y - dy + Y, Y) * X + lax.rem(x - dx + X, X) for dy, dx in STEPS])
    z_groups = [[g * Z + k for k in range(Z)] for g in range(X * Y)]

    flat = lambda array: array[0].reshape(frames, records * features)
    packed = pack_items(flat(queries), flat(key_states), flat(value_states))
    out_rows = [out_weight[0]] + [
        lax.ppermute(out_weight[0], "seq", seq_pairs(0, 0, k)) for k in range(1, Z)
    ]
    out_group = place(along_z, out_rows).reshape(-1, width)
    received = exchange(after(packed, out_group))
    grads = out_grad[0].transpose(1, 0, 2)
    inputs = layer_input[0].transpose(1, 0, 2)
    out_pieces = [out_group] + [across(out_group, *step) for step in STEPS[1:]]
    attn_grad = project(places, grads.reshape(records * frames, width), out_pieces)
    received_grads = exchange(after(attn_grad, received))

    record = seq // HEADS
    valid = jnp.sum(jnp.where(jnp.arange(records) == record, lengths[0], 0)).reshape(1)
    keys, queries_t, keys_t = prepare(valid, received)
    weights_0, sums_0 = softmax_weights(0, keys, queries_t)
    copies = jnp.broadcast_to(qkv_weight, (Z,) + qkv_weight.shape[1:])
    group = exchange(after(copies, received_grads, sums_0), z_groups).reshape(-1, qkv_weight.shape[2])
    weights_1, sums_1 = softmax_weights(1, after(keys, received_grads, sums_0), queries_t)
    rest = (queries_t, keys_t, received, received_grads)
    begun = attention_grads(0, weights_0, after(sums_0, group, sums_1), *rest)
    near = [across(group, *step) for step in NEAR]
    gradients = attention_grads(1, weights_1, after(sums_1, *near), *rest, begun)
    diagonal = [across(after(group, *near), *step) for step in DIAGONAL]
    back = exchange(after(gradients, *diagonal))
    far = [across(after(group, *diagonal), *step) for step in FAR]
    weight = place(places, [group] + near + diagonal + far).reshape(width, 3 * features)
    result = finish(back, weight, inputs, grads, norm_gain)
    count = lax.axis_size("section")
    moved = lax.ppermute(result, "section", [(i, (i - 1) % count) for i in range(count)])
    return moved.transpose(1, 0, 2)[None]


def solution(mesh):
    rows = P("section", "seq", None, None)
    in_specs = (
        rows,
        P("section", None),
        rows,
        rows,
        rows,
        rows,
        P("section", "seq", None),
        P("section", "seq", None),
        P("section", None),
    )
    return jax.shard_map(on_device, mesh=mesh, in_specs=in_specs, out_specs=rows, check_vma=False)
```

```python
import functools

import jax
import jax.numpy as jnp
from jax import lax
from jax.experimental import pallas as pl
from jax.experimental.pallas import tpu as pltpu
from jax.sharding import PartitionSpec as P

HEADS = 16
HS = 64
EPSILON = 1e-05
MASKED = -1e30
SCALE = HS**-0.5
ROW_DOT = (((1,), (1,)), ((), ()))
PLAIN_DOT = (((1,), (0,)), ((), ()))
MIB = 1024 * 1024
QB = 256
UNIT = 96
KB = 256
UNROLL1 = True
UNROLL2 = True
Y, X, Z = 4, 2, 8
BF16 = jnp.bfloat16
F32 = jnp.float32
WHOLE = pl.BlockSpec(memory_space=pltpu.VMEM)


def cost(flops, moved, exps=0):
    return pl.CostEstimate(flops=flops, bytes_accessed=moved, transcendentals=exps)


def halves(even, odd):
    first = jnp.concatenate([even[:, :HS], odd[:, :HS]], axis=1)
    second = jnp.concatenate([even[:, HS:], odd[:, HS:]], axis=1)
    return first, second


def seq_pairs(dy, dx, dz):
    pairs = []
    for y in range(Y):
        for x in range(X):
            for z in range(Z):
                to = ((y + dy) % Y) * X * Z + ((x + dx) % X) * Z + (z + dz) % Z
                pairs.append((y * X * Z + x * Z + z, to))
    return pairs


def pack_kernel(q_ref, k_ref, v_ref, out_ref):
    half = q_ref.shape[0] // 2
    for n, ref in enumerate((q_ref, k_ref, v_ref)):
        for pair in range(ref.shape[1] // 128):
            tile = ref[:, pair * 128 : (pair + 1) * 128]
            first, second = halves(tile[:half], tile[half:])
            out_ref[2 * pair, n * half : (n + 1) * half, :] = first
            out_ref[2 * pair + 1, n * half : (n + 1) * half, :] = second


def pack_items(q, k, v):
    frames, lanes = q.shape
    out = jax.ShapeDtypeStruct((lanes // HS, 3 * frames // 2, 128), BF16)
    return pl.pallas_call(
        pack_kernel,
        out_shape=out,
        in_specs=[WHOLE] * 3,
        out_specs=WHOLE,
        compiler_params=pltpu.CompilerParams(vmem_limit_bytes=16 * MIB),
        cost_estimate=cost(0, 3 * MIB),
    )(q, k, v)


def project_kernel(owner_ref, grad_ref, *refs):
    out_ref = refs[-1]
    records = grad_ref.shape[0] // 64
    grads = grad_ref[...]
    for n, ref in enumerate(refs[:-1]):
        owner = owner_ref[n]
        tile = lax.dot_general(grads, ref[...], ROW_DOT, preferred_element_type=F32).astype(BF16)
        for r in range(records):
            first, second = halves(tile[r * 64 : r * 64 + 32], tile[r * 64 + 32 : r * 64 + 64])
            out_ref[r * HEADS + 2 * owner] = first
            out_ref[r * HEADS + 2 * owner + 1] = second


def project(owners, grads, pieces):
    rows, width = grads.shape
    items = (rows // 64) * HEADS
    return pl.pallas_call(
        project_kernel,
        out_shape=jax.ShapeDtypeStruct((items, 32, 128), BF16),
        in_specs=[pl.BlockSpec(memory_space=pltpu.SMEM)] + [WHOLE] * (1 + len(pieces)),
        out_specs=WHOLE,
        compiler_params=pltpu.CompilerParams(vmem_limit_bytes=20 * MIB),
        cost_estimate=cost(2 * rows * width * 1024, 2 * (rows * width + 1024 * width + rows * 1024)),
    )(owners, grads, *pieces)


def fold(values, op):
    return op(values.reshape(values.shape[0] // 8, 8, values.shape[1]), axis=0)


def prepare_kernel(length_ref, r_ref, kz_ref, qt_ref, kt_ref):
    sources = r_ref.shape[0]
    rows = sources * 32
    length = 2 * rows
    valid = length_ref[0]
    packed_q = r_ref[:, 0:32, :].reshape(rows, 128)
    packed_k = r_ref[:, 32:64, :].reshape(rows, 128)
    q_turned = packed_q.T
    k_turned = packed_k.T
    for half in range(2):
        qt_ref[0:HS, half * rows : (half + 1) * rows] = q_turned[half * HS : (half + 1) * HS, :]
        kt_ref[:, half * rows : (half + 1) * rows] = k_turned[half * HS : (half + 1) * HS, :]
    row_id = lax.broadcasted_iota(jnp.int32, (HS, length), 0)
    qt_ref[HS:128, :] = jnp.where(row_id == 0, 1.0, 0.0).astype(BF16)
    spot = lax.broadcasted_iota(jnp.int32, (rows, HS), 0)
    lane = lax.broadcasted_iota(jnp.int32, (rows, HS), 1)
    for half in range(2):
        frame = (spot // 32) * 64 + half * 32 + spot % 32
        bias = jnp.where((lane == 0) & (frame >= valid), MASKED, 0.0).astype(BF16)
        keys = packed_k[:, half * HS : (half + 1) * HS] * SCALE
        kz_ref[half * rows : (half + 1) * rows, :] = jnp.concatenate([keys.astype(BF16), bias], axis=1)


def prepare(valid, received):
    length = received.shape[0] * 64
    return pl.pallas_call(
        prepare_kernel,
        out_shape=[
            jax.ShapeDtypeStruct((length, 128), BF16),
            jax.ShapeDtypeStruct((128, length), BF16),
            jax.ShapeDtypeStruct((HS, length), BF16),
        ],
        in_specs=[pl.BlockSpec(memory_space=pltpu.SMEM), WHOLE],
        out_specs=[WHOLE] * 3,
        compiler_params=pltpu.CompilerParams(vmem_limit_bytes=16 * MIB),
        cost_estimate=cost(0, 4 * MIB),
    )(valid, received)


def weights_kernel(gate_ref, kz_ref, qt_ref, w_ref, l_ref, s_ref):
    length = kz_ref.shape[0]
    queries = qt_ref[...]

    def first(j, top):
        at = pl.ds(pl.multiple_of(j * KB, KB), KB)
        s = lax.dot_general(kz_ref[at, :], queries, PLAIN_DOT, preferred_element_type=F32)
        s_ref[at, :] = s
        return jnp.maximum(top, fold(s, jnp.max))

    top = lax.fori_loop(0, length // KB, first, jnp.full((8, QB), -jnp.inf, F32), unroll=UNROLL1)
    top = jnp.max(top, axis=0, keepdims=True)

    def second(j, total):
        at = pl.ds(pl.multiple_of(j * KB, KB), KB)
        w = jnp.exp(s_ref[at, :] - top)
        w_ref[0, at, :] = w
        return total + fold(w, jnp.sum)

    total = lax.fori_loop(0, length // KB, second, jnp.zeros((8, QB), F32), unroll=UNROLL1)
    l_ref[...] = jnp.sum(total, axis=0, keepdims=True)


def softmax_weights(part, gate, keys, queries_t):
    length = keys.shape[0]
    blocks = length // QB // 2
    fixed = lambda shape: pl.BlockSpec(shape, lambda i: (0,) * len(shape))
    return pl.pallas_call(
        weights_kernel,
        grid=(blocks,),
        out_shape=[
            jax.ShapeDtypeStruct((blocks, length, QB), F32),
            jax.ShapeDtypeStruct((1, length // 2), F32),
        ],
        in_specs=[
            pl.BlockSpec(memory_space=pltpu.SMEM),
            fixed(keys.shape),
            pl.BlockSpec((128, QB), lambda i: (0, part * blocks + i)),
        ],
        out_specs=[
            pl.BlockSpec((1, length, QB), lambda i: (i, 0, 0)),
            pl.BlockSpec((1, QB), lambda i: (0, i)),
        ],
        scratch_shapes=[pltpu.VMEM((length, QB), F32)],
        compiler_params=pltpu.CompilerParams(vmem_limit_bytes=24 * MIB),
        cost_estimate=cost(4 * length * length * HS, 2 * length * length, length * length // 2),
    )(gate, keys, queries_t)


def grads_kernel(part, w_ref, l_ref, qt_ref, kt_ref, r_ref, g_ref, *refs):
    if part == 0:
        dq_ref, acc_ref, gt_ref, dp_ref = refs
    else:
        begun_dq_ref, begun_ref, out_ref, gt_ref, dp_ref, acc_ref, dq_ref = refs
    step = pl.program_id(0)
    sources = r_ref.shape[0]
    rows = sources * 32
    length = 2 * rows
    per = KB // 32

    @pl.when(step == 0)
    def _():
        gt_ref[...] = g_ref[...].reshape(rows, 128).T[part * HS : (part + 1) * HS, :]
        acc_ref[...] = jnp.zeros_like(acc_ref) if part == 0 else begun_ref[...]

    here = pl.ds(pl.multiple_of(step * QB, QB), QB)
    grads = gt_ref[:, here]
    none = jnp.zeros((HS, QB), BF16)
    inverse = 1.0 / l_ref[...]

    def first(half, side, j, centre):
        at = pl.ds(pl.multiple_of(half * rows + j * KB, KB), KB)
        values = r_ref[pl.ds(j * per, per), 64:96, :].reshape(KB, 128)
        dp = lax.dot_general(values, side, PLAIN_DOT, preferred_element_type=F32)
        dp_ref[at, :] = dp
        return centre + fold(w_ref[0, at, :] * inverse * dp, jnp.sum)

    centre = jnp.zeros((8, QB), F32)
    for half in range(2):
        side = jnp.concatenate([grads, none] if half == 0 else [none, grads], axis=0)
        centre = lax.fori_loop(0, rows // KB, functools.partial(first, half, side), centre, unroll=UNROLL2)
    centre = jnp.sum(centre, axis=0, keepdims=True)

    scaled_q = (qt_ref[0:HS, :] * SCALE).astype(BF16)
    side_t = jnp.concatenate([scaled_q, none], axis=0)
    side_w = jnp.concatenate([none, grads], axis=0)

    def second(j, dqt):
        at = pl.ds(pl.multiple_of(j * KB, KB), KB)
        p = w_ref[0, at, :] * inverse
        t = (p * (dp_ref[at, :] - centre)).astype(BF16)
        acc_ref[at, :] += lax.dot_general(
            t, side_t, ROW_DOT, preferred_element_type=F32
        ) + lax.dot_general(p.astype(BF16), side_w, ROW_DOT, preferred_element_type=F32)
        return dqt + lax.dot_general(kt_ref[:, at], t, PLAIN_DOT, preferred_element_type=F32)

    dqt = lax.fori_loop(0, length // KB, second, jnp.zeros((HS, QB), F32), unroll=UNROLL2)
    dq_ref[:, here] = dqt * SCALE

    if part == 1:

        @pl.when(step == pl.num_programs(0) - 1)
        def _():
            both = jnp.concatenate([begun_dq_ref[...], dq_ref[...]], axis=0)
            out_ref[:, 0:32, :] = both.T.astype(BF16).reshape(sources, 32, 128)
            for half in range(2):
                lanes = acc_ref[half * rows : (half + 1) * rows, :].astype(BF16)
                at = slice(32 + half * 32, 64 + half * 32)
                out_ref[:, at, :] = lanes.reshape(sources, 32, 128)


def attention_grads(part, weights, sums, queries_t, keys_t, received, received_grads, begun=()):
    blocks, length, _ = weights.shape
    sources = received.shape[0]
    dq = jax.ShapeDtypeStruct((HS, length // 2), F32)
    acc = jax.ShapeDtypeStruct((length, 128), F32)
    scratch = [pltpu.VMEM((HS, length // 2), BF16), pltpu.VMEM((length, QB), F32)]
    if part == 0:
        out_shape = [dq, acc]
    else:
        out_shape = jax.ShapeDtypeStruct((sources, 96, 128), BF16)
        scratch += [pltpu.VMEM((length, 128), F32), pltpu.VMEM((HS, length // 2), F32)]
    fixed = lambda array: pl.BlockSpec(array.shape, lambda i: (0,) * len(array.shape))
    return pl.pallas_call(
        functools.partial(grads_kernel, part),
        grid=(blocks,),
        out_shape=out_shape,
        in_specs=[
            pl.BlockSpec((1, length, QB), lambda i: (i, 0, 0)),
            pl.BlockSpec((1, QB), lambda i: (0, i)),
            pl.BlockSpec((128, QB), lambda i: (0, part * blocks + i)),
        ]
        + [fixed(array) for array in (keys_t, received, received_grads, *begun)],
        out_specs=jax.tree.map(fixed, out_shape),
        scratch_shapes=scratch,
        compiler_params=pltpu.CompilerParams(vmem_limit_bytes=44 * MIB),
        cost_estimate=cost(16 * length * length * HS, 2 * length * length),
    )(weights, sums, queries_t, keys_t, received, received_grads, *begun)


def finish_kernel(start_ref, back_ref, x_ref, g_ref, gain_ref, *refs):
    pieces, (out_ref, j_ref, n_ref, w_ref, sems) = refs[:-5], refs[-5:]
    copies = []
    for n, piece in enumerate(pieces):
        to = pl.ds(pl.multiple_of(start_ref[n] * UNIT, UNIT), piece.shape[0])
        copies.append(pltpu.make_async_copy(piece, w_ref.at[to, :], sems.at[n]))
        copies[-1].start()
    records = x_ref.shape[0]
    frames = x_ref.shape[1]
    width = x_ref.shape[2]
    features = HEADS * HS
    for r in range(records):
        for pair in range(HEADS // 2):
            item = r * HEADS + 2 * pair
            at = slice(pair * 128, (pair + 1) * 128)
            first, second = halves(back_ref[item, 0:32], back_ref[item + 1, 0:32])
            j_ref[r * frames : r * frames + 32, at] = first
            j_ref[r * frames + 32 : (r + 1) * frames, at] = second
            keys, values = halves(back_ref[item, 32:96], back_ref[item + 1, 32:96])
            span = slice(r * frames, (r + 1) * frames)
            j_ref[span, features + pair * 128 : features + (pair + 1) * 128] = keys
            j_ref[span, 2 * features + pair * 128 : 2 * features + (pair + 1) * 128] = values
    for copy in copies:
        copy.wait()
    step = 256
    for n in range(width // step):
        n_ref[:, n * step : (n + 1) * step] = lax.dot_general(
            j_ref[...], w_ref[n * step : (n + 1) * step, :], ROW_DOT, preferred_element_type=F32
        )
    for r in range(records):
        x = x_ref[r].astype(F32)
        centred = x - jnp.mean(x, axis=1, keepdims=True)
        var = jnp.mean(centred * centred, axis=1, keepdims=True)
        deviation = lax.rsqrt(var + EPSILON)
        normal = centred * deviation
        scaled = n_ref[r * frames : (r + 1) * frames, :] * gain_ref[...]
        residual = deviation * (
            scaled
            - jnp.mean(scaled, axis=1, keepdims=True)
            - normal * jnp.mean(scaled * normal, axis=1, keepdims=True)
        )
        out_ref[r] = (g_ref[r].astype(F32) + residual).astype(BF16)


def finish(starts, pieces, back, inputs, grads, gain):
    records, frames, width = inputs.shape
    anywhere = pl.BlockSpec(memory_space=pltpu.HBM)
    depth = pieces[0].shape[1]
    return pl.pallas_call(
        finish_kernel,
        out_shape=jax.ShapeDtypeStruct(inputs.shape, BF16),
        in_specs=[pl.BlockSpec(memory_space=pltpu.SMEM)] + [WHOLE] * 4 + [anywhere] * len(pieces),
        out_specs=WHOLE,
        scratch_shapes=[
            pltpu.VMEM((records * frames, depth), BF16),
            pltpu.VMEM((records * frames, width), F32),
            pltpu.VMEM((width, depth), BF16),
            pltpu.SemaphoreType.DMA((len(pieces),)),
        ],
        compiler_params=pltpu.CompilerParams(vmem_limit_bytes=32 * MIB),
        cost_estimate=cost(2 * records * frames * width * depth, 2 * depth * width),
    )(starts, back, inputs, grads, gain, *pieces)


def exchange(items, groups=None):
    return lax.all_to_all(items, "seq", split_axis=0, concat_axis=0, tiled=True, axis_index_groups=groups)


def after(value, *others):
    return lax.optimization_barrier((value,) + others)[0]


def across(rows, dy, dx):
    return lax.ppermute(rows, "seq", seq_pairs(dy, dx, 0))


STEPS = ((0, 0), (0, 1), (1, 0), (3, 0), (1, 1), (3, 1), (2, 0), (2, 1))


def nearby(group):
    return [across(group, *step) for step in STEPS[1:4]]


def further(near):
    partner, below, _ = near
    return [across(partner, 1, 0), across(partner, 3, 0), across(below, 1, 0)]


def on_device(
    layer_input,
    norm_gain,
    queries,
    key_states,
    value_states,
    out_grad,
    out_weight,
    qkv_weight,
    lengths,
):
    frames, records, features = queries.shape[1:]
    width = out_grad.shape[3]
    seq = lax.axis_index("seq").astype(jnp.int32)
    y, x = seq // (X * Z), lax.rem(seq // Z, X)
    places = jnp.stack([lax.rem(y - dy + Y, Y) * X + lax.rem(x - dx + X, X) for dy, dx in STEPS])
    z_groups = [[g * Z + k for k in range(Z)] for g in range(X * Y)]

    copies = jnp.broadcast_to(out_weight, (Z,) + out_weight.shape[1:])
    out_group = exchange(copies, z_groups).reshape(-1, width)
    flat = lambda array: array[0].reshape(frames, records * features)
    packed = pack_items(flat(queries), flat(key_states), flat(value_states))
    received = exchange(after(packed, out_group))
    grads = out_grad[0].transpose(1, 0, 2)
    inputs = layer_input[0].transpose(1, 0, 2)
    near = nearby(out_group)
    far = further(near)
    out_pieces = [out_group] + near + far + [across(far[2], 0, 1)]
    attn_grad = project(places, grads.reshape(records * frames, width), out_pieces)
    received_grads = exchange(after(attn_grad, received))

    record = seq // HEADS
    valid = jnp.sum(jnp.where(jnp.arange(records) == record, lengths[0], 0)).reshape(1)
    keys, queries_t, keys_t = prepare(valid, received)
    weights_0, sums_0 = softmax_weights(0, valid, keys, queries_t)
    copies = jnp.broadcast_to(qkv_weight, (Z,) + qkv_weight.shape[1:])
    qkv_group = exchange(after(copies, received_grads, sums_0), z_groups).reshape(-1, qkv_weight.shape[2])
    weights_1, sums_1 = softmax_weights(1, after(valid, received_grads, sums_0), keys, queries_t)
    rest = (queries_t, keys_t, received, received_grads)
    begun = attention_grads(0, weights_0, after(sums_0, qkv_group, sums_1), *rest)
    near = nearby(qkv_group)
    sums_1, *near = lax.optimization_barrier((sums_1, *near))
    gradients = attention_grads(1, weights_1, sums_1, *rest, begun)
    partner, below, above = near
    diagonal = [across(partner, 1, 0), across(partner, 3, 0)]
    gradients, *diagonal = lax.optimization_barrier((gradients, *diagonal))
    back = exchange(gradients)
    far = []
    for down, up in ((below, above), tuple(diagonal)):
        far += [across(down[:UNIT], 1, 0), across(up[UNIT:], 3, 0)]
    starts = jnp.concatenate([2 * places[:6], jnp.stack([2 * places[6], 2 * places[6] + 1, 2 * places[7], 2 * places[7] + 1])])
    result = finish(starts, [qkv_group] + near + diagonal + far, back, inputs, grads, norm_gain)
    count = lax.axis_size("section")
    moved = lax.ppermute(result, "section", [(i, (i - 1) % count) for i in range(count)])
    return moved.transpose(1, 0, 2)[None]


def solution(mesh):
    rows = P("section", "seq", None, None)
    in_specs = (
        rows,
        P("section", None),
        rows,
        rows,
        rows,
        rows,
        P("section", "seq", None),
        P("section", "seq", None),
        P("section", None),
    )
    return jax.shard_map(on_device, mesh=mesh, in_specs=in_specs, out_specs=rows, check_vma=False)
```

```python
import functools

import jax
import jax.numpy as jnp
from jax import lax
from jax.experimental import pallas as pl
from jax.experimental.pallas import tpu as pltpu
from jax.sharding import PartitionSpec as P

HEADS = 16
HS = 64
EPSILON = 1e-05
MASKED = -1e30
SCALE = HS**-0.5
ROW_DOT = (((1,), (1,)), ((), ()))
PLAIN_DOT = (((1,), (0,)), ((), ()))
MIB = 1024 * 1024
QB = 256
KB = 256
UNROLL1 = True
UNROLL2 = True
Y, X, Z = 4, 2, 8
BF16 = jnp.bfloat16
F32 = jnp.float32
WHOLE = pl.BlockSpec(memory_space=pltpu.VMEM)
ROOM = 60 * MIB


def cost(flops, moved, exps=0):
    return pl.CostEstimate(flops=flops, bytes_accessed=moved, transcendentals=exps)


def fixed(array):
    return pl.BlockSpec(array.shape, lambda i: (0,) * len(array.shape))


def halves(even, odd):
    first = jnp.concatenate([even[:, :HS], odd[:, :HS]], axis=1)
    second = jnp.concatenate([even[:, HS:], odd[:, HS:]], axis=1)
    return first, second


def seq_pairs(dy, dx, dz):
    pairs = []
    for y in range(Y):
        for x in range(X):
            for z in range(Z):
                to = ((y + dy) % Y) * X * Z + ((x + dx) % X) * Z + (z + dz) % Z
                pairs.append((y * X * Z + x * Z + z, to))
    return pairs


def pack_kernel(q_ref, k_ref, v_ref, out_ref):
    half = q_ref.shape[0] // 2
    for n, ref in enumerate((q_ref, k_ref, v_ref)):
        for pair in range(ref.shape[1] // 128):
            tile = ref[:, pair * 128 : (pair + 1) * 128]
            first, second = halves(tile[:half], tile[half:])
            out_ref[2 * pair, n * half : (n + 1) * half, :] = first
            out_ref[2 * pair + 1, n * half : (n + 1) * half, :] = second


def pack_items(q, k, v):
    frames, lanes = q.shape
    out = jax.ShapeDtypeStruct((lanes // HS, 3 * frames // 2, 128), BF16)
    return pl.pallas_call(
        pack_kernel,
        out_shape=out,
        in_specs=[WHOLE] * 3,
        out_specs=WHOLE,
        compiler_params=pltpu.CompilerParams(vmem_limit_bytes=16 * MIB),
        cost_estimate=cost(0, 3 * MIB),
    )(q, k, v)


def project_kernel(owner_ref, grad_ref, *refs):
    out_ref = refs[-1]
    records = grad_ref.shape[0] // 64
    grads = grad_ref[...]
    for n, ref in enumerate(refs[:-1]):
        owner = owner_ref[n]
        tile = lax.dot_general(grads, ref[...], ROW_DOT, preferred_element_type=F32).astype(BF16)
        for r in range(records):
            first, second = halves(tile[r * 64 : r * 64 + 32], tile[r * 64 + 32 : r * 64 + 64])
            out_ref[r * HEADS + 2 * owner] = first
            out_ref[r * HEADS + 2 * owner + 1] = second


def project(owners, grads, pieces):
    rows, width = grads.shape
    items = (rows // 64) * HEADS
    return pl.pallas_call(
        project_kernel,
        out_shape=jax.ShapeDtypeStruct((items, 32, 128), BF16),
        in_specs=[pl.BlockSpec(memory_space=pltpu.SMEM)] + [WHOLE] * (1 + len(pieces)),
        out_specs=WHOLE,
        compiler_params=pltpu.CompilerParams(vmem_limit_bytes=20 * MIB),
        cost_estimate=cost(2 * rows * width * 1024, 2 * (rows * width + 1024 * width + rows * 1024)),
    )(owners, grads, *pieces)


def fold(values, op):
    return op(values.reshape(values.shape[0] // 8, 8, values.shape[1]), axis=0)


def prepare_kernel(length_ref, r_ref, kz_ref, qt_ref, kt_ref):
    sources = r_ref.shape[0]
    rows = sources * 32
    length = 2 * rows
    valid = length_ref[0]
    packed_q = r_ref[:, 0:32, :].reshape(rows, 128)
    packed_k = r_ref[:, 32:64, :].reshape(rows, 128)
    q_turned = packed_q.T
    k_turned = packed_k.T
    for half in range(2):
        qt_ref[0:HS, half * rows : (half + 1) * rows] = q_turned[half * HS : (half + 1) * HS, :]
        kt_ref[:, half * rows : (half + 1) * rows] = k_turned[half * HS : (half + 1) * HS, :]
    row_id = lax.broadcasted_iota(jnp.int32, (HS, length), 0)
    qt_ref[HS:128, :] = jnp.where(row_id == 0, 1.0, 0.0).astype(BF16)
    spot = lax.broadcasted_iota(jnp.int32, (rows, HS), 0)
    lane = lax.broadcasted_iota(jnp.int32, (rows, HS), 1)
    for half in range(2):
        frame = (spot // 32) * 64 + half * 32 + spot % 32
        bias = jnp.where((lane == 0) & (frame >= valid), MASKED, 0.0).astype(BF16)
        keys = packed_k[:, half * HS : (half + 1) * HS] * SCALE
        kz_ref[half * rows : (half + 1) * rows, :] = jnp.concatenate([keys.astype(BF16), bias], axis=1)


def prepare(valid, received):
    length = received.shape[0] * 64
    out_shape = [
        jax.ShapeDtypeStruct((length, 128), BF16),
        jax.ShapeDtypeStruct((128, length), BF16),
        jax.ShapeDtypeStruct((HS, length), BF16),
    ]
    return pl.pallas_call(
        prepare_kernel,
        grid=(1,),
        out_shape=out_shape,
        in_specs=[pl.BlockSpec(memory_space=pltpu.SMEM), fixed(received)],
        out_specs=[fixed(shape) for shape in out_shape],
        compiler_params=pltpu.CompilerParams(vmem_limit_bytes=ROOM),
        cost_estimate=cost(0, 4 * MIB),
    )(valid, received)


def weights_kernel(gate_ref, kz_ref, qt_ref, w_ref, l_ref, s_ref):
    length = kz_ref.shape[0]
    queries = qt_ref[...]

    def first(j, top):
        at = pl.ds(pl.multiple_of(j * KB, KB), KB)
        s = lax.dot_general(kz_ref[at, :], queries, PLAIN_DOT, preferred_element_type=F32)
        s_ref[at, :] = s
        return jnp.maximum(top, fold(s, jnp.max))

    top = lax.fori_loop(0, length // KB, first, jnp.full((8, QB), -jnp.inf, F32), unroll=UNROLL1)
    top = jnp.max(top, axis=0, keepdims=True)

    def second(j, total):
        at = pl.ds(pl.multiple_of(j * KB, KB), KB)
        w = jnp.exp(s_ref[at, :] - top)
        w_ref[0, at, :] = w
        return total + fold(w, jnp.sum)

    total = lax.fori_loop(0, length // KB, second, jnp.zeros((8, QB), F32), unroll=UNROLL1)
    l_ref[...] = jnp.sum(total, axis=0, keepdims=True)


def softmax_weights(part, gate, keys, queries_t):
    length = keys.shape[0]
    blocks = length // QB // 2
    return pl.pallas_call(
        weights_kernel,
        grid=(blocks,),
        out_shape=[
            jax.ShapeDtypeStruct((blocks, length, QB), F32),
            jax.ShapeDtypeStruct((1, length // 2), F32),
        ],
        in_specs=[
            pl.BlockSpec(memory_space=pltpu.SMEM),
            fixed(keys),
            pl.BlockSpec((128, QB), lambda i: (0, part * blocks + i)),
        ],
        out_specs=[
            pl.BlockSpec((1, length, QB), lambda i: (i, 0, 0)),
            pl.BlockSpec((1, QB), lambda i: (0, i)),
        ],
        scratch_shapes=[pltpu.VMEM((length, QB), F32)],
        compiler_params=pltpu.CompilerParams(vmem_limit_bytes=ROOM),
        cost_estimate=cost(4 * length * length * HS, 2 * length * length, length * length // 2),
    )(gate, keys, queries_t)


def grads_kernel(part, w_ref, l_ref, qt_ref, kt_ref, r_ref, g_ref, *refs):
    if part == 0:
        dq_ref, acc_ref, gt_ref, dp_ref = refs
    else:
        begun_dq_ref, begun_ref, out_ref, gt_ref, dp_ref, acc_ref, dq_ref = refs
    step = pl.program_id(0)
    sources = r_ref.shape[0]
    rows = sources * 32
    length = 2 * rows
    per = KB // 32

    @pl.when(step == 0)
    def _():
        gt_ref[...] = g_ref[...].reshape(rows, 128).T[part * HS : (part + 1) * HS, :]
        acc_ref[...] = jnp.zeros_like(acc_ref) if part == 0 else begun_ref[...]

    here = pl.ds(pl.multiple_of(step * QB, QB), QB)
    grads = gt_ref[:, here]
    none = jnp.zeros((HS, QB), BF16)
    inverse = 1.0 / l_ref[...]

    def first(half, side, j, centre):
        at = pl.ds(pl.multiple_of(half * rows + j * KB, KB), KB)
        values = r_ref[pl.ds(j * per, per), 64:96, :].reshape(KB, 128)
        dp = lax.dot_general(values, side, PLAIN_DOT, preferred_element_type=F32)
        dp_ref[at, :] = dp
        return centre + fold(w_ref[0, at, :] * inverse * dp, jnp.sum)

    centre = jnp.zeros((8, QB), F32)
    for half in range(2):
        side = jnp.concatenate([grads, none] if half == 0 else [none, grads], axis=0)
        centre = lax.fori_loop(0, rows // KB, functools.partial(first, half, side), centre, unroll=UNROLL2)
    centre = jnp.sum(centre, axis=0, keepdims=True)

    scaled_q = (qt_ref[0:HS, :] * SCALE).astype(BF16)
    side_t = jnp.concatenate([scaled_q, none], axis=0)
    side_w = jnp.concatenate([none, grads], axis=0)

    def second(j, dqt):
        at = pl.ds(pl.multiple_of(j * KB, KB), KB)
        p = w_ref[0, at, :] * inverse
        t = (p * (dp_ref[at, :] - centre)).astype(BF16)
        acc_ref[at, :] += lax.dot_general(
            t, side_t, ROW_DOT, preferred_element_type=F32
        ) + lax.dot_general(p.astype(BF16), side_w, ROW_DOT, preferred_element_type=F32)
        return dqt + lax.dot_general(kt_ref[:, at], t, PLAIN_DOT, preferred_element_type=F32)

    dqt = lax.fori_loop(0, length // KB, second, jnp.zeros((HS, QB), F32), unroll=UNROLL2)
    dq_ref[:, here] = dqt * SCALE

    if part == 1:

        @pl.when(step == pl.num_programs(0) - 1)
        def _():
            both = jnp.concatenate([begun_dq_ref[...], dq_ref[...]], axis=0)
            out_ref[:, 0:32, :] = both.T.astype(BF16).reshape(sources, 32, 128)
            for half in range(2):
                lanes = acc_ref[half * rows : (half + 1) * rows, :].astype(BF16)
                at = slice(32 + half * 32, 64 + half * 32)
                out_ref[:, at, :] = lanes.reshape(sources, 32, 128)


def attention_grads(part, weights, sums, queries_t, keys_t, received, received_grads, begun=()):
    blocks, length, _ = weights.shape
    sources = received.shape[0]
    dq = jax.ShapeDtypeStruct((HS, length // 2), F32)
    acc = jax.ShapeDtypeStruct((length, 128), F32)
    scratch = [pltpu.VMEM((HS, length // 2), BF16), pltpu.VMEM((length, QB), F32)]
    if part == 0:
        out_shape = [dq, acc]
    else:
        out_shape = jax.ShapeDtypeStruct((sources, 96, 128), BF16)
        scratch += [pltpu.VMEM((length, 128), F32), pltpu.VMEM((HS, length // 2), F32)]
    return pl.pallas_call(
        functools.partial(grads_kernel, part),
        grid=(blocks,),
        out_shape=out_shape,
        in_specs=[
            pl.BlockSpec((1, length, QB), lambda i: (i, 0, 0)),
            pl.BlockSpec((1, QB), lambda i: (0, i)),
            pl.BlockSpec((128, QB), lambda i: (0, part * blocks + i)),
        ]
        + [fixed(array) for array in (keys_t, received, received_grads, *begun)],
        out_specs=jax.tree.map(fixed, out_shape),
        scratch_shapes=scratch,
        compiler_params=pltpu.CompilerParams(vmem_limit_bytes=ROOM),
        cost_estimate=cost(16 * length * length * HS, 2 * length * length),
    )(weights, sums, queries_t, keys_t, received, received_grads, *begun)


def finish_kernel(owner_ref, back_ref, x_ref, g_ref, gain_ref, *refs):
    pieces, (out_ref, j_ref, n_ref, w_ref, sems) = refs[:-5], refs[-5:]
    copies = []
    for n, piece in enumerate(pieces):
        rows = piece.shape[0]
        to = pl.ds(pl.multiple_of(owner_ref[n] * rows, rows), rows)
        copies.append(pltpu.make_async_copy(piece, w_ref.at[to, :], sems.at[n]))
        copies[-1].start()
    records = x_ref.shape[0]
    frames = x_ref.shape[1]
    width = x_ref.shape[2]
    features = HEADS * HS
    for r in range(records):
        for pair in range(HEADS // 2):
            item = r * HEADS + 2 * pair
            at = slice(pair * 128, (pair + 1) * 128)
            first, second = halves(back_ref[item, 0:32], back_ref[item + 1, 0:32])
            j_ref[r * frames : r * frames + 32, at] = first
            j_ref[r * frames + 32 : (r + 1) * frames, at] = second
            keys, values = halves(back_ref[item, 32:96], back_ref[item + 1, 32:96])
            span = slice(r * frames, (r + 1) * frames)
            j_ref[span, features + pair * 128 : features + (pair + 1) * 128] = keys
            j_ref[span, 2 * features + pair * 128 : 2 * features + (pair + 1) * 128] = values
    for copy in copies:
        copy.wait()
    step = 256
    for n in range(width // step):
        n_ref[:, n * step : (n + 1) * step] = lax.dot_general(
            j_ref[...], w_ref[n * step : (n + 1) * step, :], ROW_DOT, preferred_element_type=F32
        )
    for r in range(records):
        x = x_ref[r].astype(F32)
        centred = x - jnp.mean(x, axis=1, keepdims=True)
        var = jnp.mean(centred * centred, axis=1, keepdims=True)
        deviation = lax.rsqrt(var + EPSILON)
        normal = centred * deviation
        scaled = n_ref[r * frames : (r + 1) * frames, :] * gain_ref[...]
        residual = deviation * (
            scaled
            - jnp.mean(scaled, axis=1, keepdims=True)
            - normal * jnp.mean(scaled * normal, axis=1, keepdims=True)
        )
        out_ref[r] = (g_ref[r].astype(F32) + residual).astype(BF16)


def finish(owners, pieces, back, inputs, grads, gain):
    records, frames, width = inputs.shape
    anywhere = pl.BlockSpec(memory_space=pltpu.HBM)
    depth = pieces[0].shape[1]
    return pl.pallas_call(
        finish_kernel,
        grid=(1,),
        out_shape=jax.ShapeDtypeStruct(inputs.shape, BF16),
        in_specs=[pl.BlockSpec(memory_space=pltpu.SMEM)]
        + [fixed(array) for array in (back, inputs, grads, gain)]
        + [anywhere] * len(pieces),
        out_specs=fixed(inputs),
        scratch_shapes=[
            pltpu.VMEM((records * frames, depth), BF16),
            pltpu.VMEM((records * frames, width), F32),
            pltpu.VMEM((width, depth), BF16),
            pltpu.SemaphoreType.DMA((len(pieces),)),
        ],
        compiler_params=pltpu.CompilerParams(vmem_limit_bytes=ROOM),
        cost_estimate=cost(2 * records * frames * width * depth, 2 * depth * width),
    )(owners, back, inputs, grads, gain, *pieces)


def exchange(items, groups=None):
    return lax.all_to_all(items, "seq", split_axis=0, concat_axis=0, tiled=True, axis_index_groups=groups)


def after(value, *others):
    return lax.optimization_barrier((value,) + others)[0]


def across(rows, dy, dx):
    return lax.ppermute(rows, "seq", seq_pairs(dy, dx, 0))


STEPS = ((0, 0), (0, 1), (1, 0), (3, 0), (1, 1), (3, 1), (2, 0), (2, 1))


def nearby(group):
    return [across(group, *step) for step in STEPS[1:4]]


def further(near):
    partner, below, _ = near
    return [across(partner, 1, 0), across(partner, 3, 0), across(below, 1, 0)]


def on_device(
    layer_input,
    norm_gain,
    queries,
    key_states,
    value_states,
    out_grad,
    out_weight,
    qkv_weight,
    lengths,
):
    frames, records, features = queries.shape[1:]
    width = out_grad.shape[3]
    seq = lax.axis_index("seq").astype(jnp.int32)
    y, x = seq // (X * Z), lax.rem(seq // Z, X)
    places = jnp.stack([lax.rem(y - dy + Y, Y) * X + lax.rem(x - dx + X, X) for dy, dx in STEPS])
    z_groups = [[g * Z + k for k in range(Z)] for g in range(X * Y)]

    copies = jnp.broadcast_to(out_weight, (Z,) + out_weight.shape[1:])
    out_group = exchange(copies, z_groups).reshape(-1, width)
    flat = lambda array: array[0].reshape(frames, records * features)
    packed = pack_items(flat(queries), flat(key_states), flat(value_states))
    received = exchange(after(packed, out_group))
    grads = out_grad[0].transpose(1, 0, 2)
    inputs = layer_input[0].transpose(1, 0, 2)
    near = nearby(out_group)
    far = further(near)
    out_pieces = [out_group] + near + far + [across(far[2], 0, 1)]
    attn_grad = project(places, grads.reshape(records * frames, width), out_pieces)
    received_grads = exchange(after(attn_grad, received))

    record = seq // HEADS
    valid = jnp.sum(jnp.where(jnp.arange(records) == record, lengths[0], 0)).reshape(1)
    keys, queries_t, keys_t = prepare(valid, received)
    weights_0, sums_0 = softmax_weights(0, valid, keys, queries_t)
    copies = jnp.broadcast_to(qkv_weight, (Z,) + qkv_weight.shape[1:])
    qkv_group = exchange(after(copies, received_grads, sums_0), z_groups).reshape(-1, qkv_weight.shape[2])
    weights_1, sums_1 = softmax_weights(1, after(valid, received_grads, sums_0), keys, queries_t)
    rest = (queries_t, keys_t, received, received_grads)
    begun = attention_grads(0, weights_0, after(sums_0, qkv_group, sums_1), *rest)
    near = nearby(qkv_group)
    sums_1, *near = lax.optimization_barrier((sums_1, *near))
    gradients = attention_grads(1, weights_1, sums_1, *rest, begun)
    partner, below, above = near
    diagonal = [across(partner, 1, 0), across(partner, 3, 0)]
    gradients, *diagonal = lax.optimization_barrier((gradients, *diagonal))
    back = exchange(gradients)
    far = [across(after(below, gradients), 1, 0), across(diagonal[1], 3, 0)]
    result = finish(places, [qkv_group] + near + diagonal + far, back, inputs, grads, norm_gain)
    count = lax.axis_size("section")
    moved = lax.ppermute(result, "section", [(i, (i - 1) % count) for i in range(count)])
    return moved.transpose(1, 0, 2)[None]


def solution(mesh):
    rows = P("section", "seq", None, None)
    in_specs = (
        rows,
        P("section", None),
        rows,
        rows,
        rows,
        rows,
        P("section", "seq", None),
        P("section", "seq", None),
        P("section", None),
    )
    return jax.shard_map(on_device, mesh=mesh, in_specs=in_specs, out_specs=rows, check_vma=False)
```

```python
import functools

import jax
import jax.numpy as jnp
from jax import lax
from jax.experimental import pallas as pl
from jax.experimental.pallas import tpu as pltpu
from jax.sharding import PartitionSpec as P

HEADS = 16
HS = 64
EPSILON = 1e-05
MASKED = -1e30
SCALE = HS**-0.5
ROW_DOT = (((1,), (1,)), ((), ()))
PLAIN_DOT = (((1,), (0,)), ((), ()))
MIB = 1024 * 1024
QB = 256
KB = 256
UNROLL1 = True
UNROLL2 = True
Y, X, Z = 4, 2, 8
BF16 = jnp.bfloat16
F32 = jnp.float32
WHOLE = pl.BlockSpec(memory_space=pltpu.VMEM)
ROOM = 60 * MIB


def cost(flops, moved, exps=0):
    return pl.CostEstimate(flops=flops, bytes_accessed=moved, transcendentals=exps)


def fixed(array):
    return pl.BlockSpec(array.shape, lambda i: (0,) * len(array.shape))


def halves(even, odd):
    first = jnp.concatenate([even[:, :HS], odd[:, :HS]], axis=1)
    second = jnp.concatenate([even[:, HS:], odd[:, HS:]], axis=1)
    return first, second


def seq_pairs(dy, dx, dz):
    pairs = []
    for y in range(Y):
        for x in range(X):
            for z in range(Z):
                to = ((y + dy) % Y) * X * Z + ((x + dx) % X) * Z + (z + dz) % Z
                pairs.append((y * X * Z + x * Z + z, to))
    return pairs


def pack_kernel(*refs):
    out_ref = refs[-1]
    half = refs[0].shape[0] // 2
    for n, ref in enumerate(refs[:-1]):
        for pair in range(ref.shape[1] // 128):
            tile = ref[:, pair * 128 : (pair + 1) * 128]
            first, second = halves(tile[:half], tile[half:])
            out_ref[2 * pair, n * half : (n + 1) * half, :] = first
            out_ref[2 * pair + 1, n * half : (n + 1) * half, :] = second


def pack_items(*arrays):
    frames, lanes = arrays[0].shape
    count = len(arrays)
    return pl.pallas_call(
        pack_kernel,
        out_shape=jax.ShapeDtypeStruct((lanes // HS, count * frames // 2, 128), BF16),
        in_specs=[WHOLE] * count,
        out_specs=WHOLE,
        compiler_params=pltpu.CompilerParams(vmem_limit_bytes=16 * MIB),
        cost_estimate=cost(0, count * MIB),
    )(*arrays)


def project_kernel(owner_ref, grad_ref, *refs):
    out_ref = refs[-1]
    records = grad_ref.shape[0] // 64
    grads = grad_ref[...]
    for n, ref in enumerate(refs[:-1]):
        owner = owner_ref[n]
        tile = lax.dot_general(grads, ref[...], ROW_DOT, preferred_element_type=F32).astype(BF16)
        for r in range(records):
            first, second = halves(tile[r * 64 : r * 64 + 32], tile[r * 64 + 32 : r * 64 + 64])
            out_ref[r * HEADS + 2 * owner] = first
            out_ref[r * HEADS + 2 * owner + 1] = second


def project(owners, grads, pieces):
    rows, width = grads.shape
    items = (rows // 64) * HEADS
    return pl.pallas_call(
        project_kernel,
        out_shape=jax.ShapeDtypeStruct((items, 32, 128), BF16),
        in_specs=[pl.BlockSpec(memory_space=pltpu.SMEM)] + [WHOLE] * (1 + len(pieces)),
        out_specs=WHOLE,
        compiler_params=pltpu.CompilerParams(vmem_limit_bytes=20 * MIB),
        cost_estimate=cost(2 * rows * width * 1024, 2 * (rows * width + 1024 * width + rows * 1024)),
    )(owners, grads, *pieces)


def fold(values, op):
    return op(values.reshape(values.shape[0] // 8, 8, values.shape[1]), axis=0)


def prepare_kernel(length_ref, r_ref, kz_ref, qt_ref, kt_ref):
    sources = r_ref.shape[0]
    rows = sources * 32
    length = 2 * rows
    valid = length_ref[0]
    packed_q = r_ref[:, 0:32, :].reshape(rows, 128)
    packed_k = r_ref[:, 32:64, :].reshape(rows, 128)
    q_turned = packed_q.T
    k_turned = packed_k.T
    for half in range(2):
        qt_ref[0:HS, half * rows : (half + 1) * rows] = q_turned[half * HS : (half + 1) * HS, :]
        kt_ref[:, half * rows : (half + 1) * rows] = k_turned[half * HS : (half + 1) * HS, :]
    row_id = lax.broadcasted_iota(jnp.int32, (HS, length), 0)
    qt_ref[HS:128, :] = jnp.where(row_id == 0, 1.0, 0.0).astype(BF16)
    spot = lax.broadcasted_iota(jnp.int32, (rows, HS), 0)
    lane = lax.broadcasted_iota(jnp.int32, (rows, HS), 1)
    for half in range(2):
        frame = (spot // 32) * 64 + half * 32 + spot % 32
        bias = jnp.where((lane == 0) & (frame >= valid), MASKED, 0.0).astype(BF16)
        keys = packed_k[:, half * HS : (half + 1) * HS] * SCALE
        kz_ref[half * rows : (half + 1) * rows, :] = jnp.concatenate([keys.astype(BF16), bias], axis=1)


def prepare(valid, received):
    length = received.shape[0] * 64
    out_shape = [
        jax.ShapeDtypeStruct((length, 128), BF16),
        jax.ShapeDtypeStruct((128, length), BF16),
        jax.ShapeDtypeStruct((HS, length), BF16),
    ]
    return pl.pallas_call(
        prepare_kernel,
        grid=(1,),
        out_shape=out_shape,
        in_specs=[pl.BlockSpec(memory_space=pltpu.SMEM), fixed(received)],
        out_specs=[fixed(shape) for shape in out_shape],
        compiler_params=pltpu.CompilerParams(vmem_limit_bytes=ROOM),
        cost_estimate=cost(0, 4 * MIB),
    )(valid, received)


def weights_kernel(gate_ref, kz_ref, qt_ref, w_ref, l_ref, s_ref):
    length = kz_ref.shape[0]
    queries = qt_ref[...]

    def first(j, top):
        at = pl.ds(pl.multiple_of(j * KB, KB), KB)
        s = lax.dot_general(kz_ref[at, :], queries, PLAIN_DOT, preferred_element_type=F32)
        s_ref[at, :] = s
        return jnp.maximum(top, fold(s, jnp.max))

    top = lax.fori_loop(0, length // KB, first, jnp.full((8, QB), -jnp.inf, F32), unroll=UNROLL1)
    top = jnp.max(top, axis=0, keepdims=True)

    def second(j, total):
        at = pl.ds(pl.multiple_of(j * KB, KB), KB)
        w = jnp.exp(s_ref[at, :] - top)
        w_ref[0, at, :] = w
        return total + fold(w, jnp.sum)

    total = lax.fori_loop(0, length // KB, second, jnp.zeros((8, QB), F32), unroll=UNROLL1)
    l_ref[...] = jnp.sum(total, axis=0, keepdims=True)


def softmax_weights(part, gate, keys, queries_t):
    length = keys.shape[0]
    blocks = length // QB // 2
    return pl.pallas_call(
        weights_kernel,
        grid=(blocks,),
        out_shape=[
            jax.ShapeDtypeStruct((blocks, length, QB), F32),
            jax.ShapeDtypeStruct((1, length // 2), F32),
        ],
        in_specs=[
            pl.BlockSpec(memory_space=pltpu.SMEM),
            fixed(keys),
            pl.BlockSpec((128, QB), lambda i: (0, part * blocks + i)),
        ],
        out_specs=[
            pl.BlockSpec((1, length, QB), lambda i: (i, 0, 0)),
            pl.BlockSpec((1, QB), lambda i: (0, i)),
        ],
        scratch_shapes=[pltpu.VMEM((length, QB), F32)],
        compiler_params=pltpu.CompilerParams(vmem_limit_bytes=ROOM),
        cost_estimate=cost(4 * length * length * HS, 2 * length * length, length * length // 2),
    )(gate, keys, queries_t)


def grads_kernel(part, w_ref, l_ref, qt_ref, kt_ref, r_ref, g_ref, *refs):
    if part == 0:
        dq_ref, acc_ref, gt_ref, dp_ref = refs
    else:
        begun_dq_ref, begun_ref, out_ref, gt_ref, dp_ref, acc_ref, dq_ref = refs
    step = pl.program_id(0)
    sources = r_ref.shape[0]
    rows = sources * 32
    length = 2 * rows
    per = KB // 32

    @pl.when(step == 0)
    def _():
        gt_ref[...] = g_ref[...].reshape(rows, 128).T[part * HS : (part + 1) * HS, :]
        acc_ref[...] = jnp.zeros_like(acc_ref) if part == 0 else begun_ref[...]

    here = pl.ds(pl.multiple_of(step * QB, QB), QB)
    grads = gt_ref[:, here]
    none = jnp.zeros((HS, QB), BF16)
    inverse = 1.0 / l_ref[...]

    def first(half, side, j, centre):
        at = pl.ds(pl.multiple_of(half * rows + j * KB, KB), KB)
        values = r_ref[pl.ds(j * per, per), :, :].reshape(KB, 128)
        dp = lax.dot_general(values, side, PLAIN_DOT, preferred_element_type=F32)
        dp_ref[at, :] = dp
        return centre + fold(w_ref[0, at, :] * inverse * dp, jnp.sum)

    centre = jnp.zeros((8, QB), F32)
    for half in range(2):
        side = jnp.concatenate([grads, none] if half == 0 else [none, grads], axis=0)
        centre = lax.fori_loop(0, rows // KB, functools.partial(first, half, side), centre, unroll=UNROLL2)
    centre = jnp.sum(centre, axis=0, keepdims=True)

    scaled_q = (qt_ref[0:HS, :] * SCALE).astype(BF16)
    side_t = jnp.concatenate([scaled_q, none], axis=0)
    side_w = jnp.concatenate([none, grads], axis=0)

    def second(j, dqt):
        at = pl.ds(pl.multiple_of(j * KB, KB), KB)
        p = w_ref[0, at, :] * inverse
        t = (p * (dp_ref[at, :] - centre)).astype(BF16)
        acc_ref[at, :] += lax.dot_general(
            t, side_t, ROW_DOT, preferred_element_type=F32
        ) + lax.dot_general(p.astype(BF16), side_w, ROW_DOT, preferred_element_type=F32)
        return dqt + lax.dot_general(kt_ref[:, at], t, PLAIN_DOT, preferred_element_type=F32)

    dqt = lax.fori_loop(0, length // KB, second, jnp.zeros((HS, QB), F32), unroll=UNROLL2)
    dq_ref[:, here] = dqt * SCALE

    if part == 1:

        @pl.when(step == pl.num_programs(0) - 1)
        def _():
            both = jnp.concatenate([begun_dq_ref[...], dq_ref[...]], axis=0)
            out_ref[:, 0:32, :] = both.T.astype(BF16).reshape(sources, 32, 128)
            for half in range(2):
                lanes = acc_ref[half * rows : (half + 1) * rows, :].astype(BF16)
                at = slice(32 + half * 32, 64 + half * 32)
                out_ref[:, at, :] = lanes.reshape(sources, 32, 128)


def attention_grads(part, weights, sums, queries_t, keys_t, received, received_grads, begun=()):
    blocks, length, _ = weights.shape
    sources = received.shape[0]
    dq = jax.ShapeDtypeStruct((HS, length // 2), F32)
    acc = jax.ShapeDtypeStruct((length, 128), F32)
    scratch = [pltpu.VMEM((HS, length // 2), BF16), pltpu.VMEM((length, QB), F32)]
    if part == 0:
        out_shape = [dq, acc]
    else:
        out_shape = jax.ShapeDtypeStruct((sources, 96, 128), BF16)
        scratch += [pltpu.VMEM((length, 128), F32), pltpu.VMEM((HS, length // 2), F32)]
    return pl.pallas_call(
        functools.partial(grads_kernel, part),
        grid=(blocks,),
        out_shape=out_shape,
        in_specs=[
            pl.BlockSpec((1, length, QB), lambda i: (i, 0, 0)),
            pl.BlockSpec((1, QB), lambda i: (0, i)),
            pl.BlockSpec((128, QB), lambda i: (0, part * blocks + i)),
        ]
        + [fixed(array) for array in (keys_t, received, received_grads, *begun)],
        out_specs=jax.tree.map(fixed, out_shape),
        scratch_shapes=scratch,
        compiler_params=pltpu.CompilerParams(vmem_limit_bytes=ROOM),
        cost_estimate=cost(16 * length * length * HS, 2 * length * length),
    )(weights, sums, queries_t, keys_t, received, received_grads, *begun)


def finish_kernel(owner_ref, back_ref, x_ref, g_ref, gain_ref, *refs):
    pieces, (out_ref, j_ref, n_ref, w_ref, sems) = refs[:-5], refs[-5:]
    copies = []
    for n, piece in enumerate(pieces):
        rows = piece.shape[0]
        to = pl.ds(pl.multiple_of(owner_ref[n] * rows, rows), rows)
        copies.append(pltpu.make_async_copy(piece, w_ref.at[to, :], sems.at[n]))
        copies[-1].start()
    records = x_ref.shape[0]
    frames = x_ref.shape[1]
    width = x_ref.shape[2]
    features = HEADS * HS
    for r in range(records):
        for pair in range(HEADS // 2):
            item = r * HEADS + 2 * pair
            at = slice(pair * 128, (pair + 1) * 128)
            first, second = halves(back_ref[item, 0:32], back_ref[item + 1, 0:32])
            j_ref[r * frames : r * frames + 32, at] = first
            j_ref[r * frames + 32 : (r + 1) * frames, at] = second
            keys, values = halves(back_ref[item, 32:96], back_ref[item + 1, 32:96])
            span = slice(r * frames, (r + 1) * frames)
            j_ref[span, features + pair * 128 : features + (pair + 1) * 128] = keys
            j_ref[span, 2 * features + pair * 128 : 2 * features + (pair + 1) * 128] = values
    for copy in copies:
        copy.wait()
    step = 256
    for n in range(width // step):
        n_ref[:, n * step : (n + 1) * step] = lax.dot_general(
            j_ref[...], w_ref[n * step : (n + 1) * step, :], ROW_DOT, preferred_element_type=F32
        )
    for r in range(records):
        x = x_ref[r].astype(F32)
        centred = x - jnp.mean(x, axis=1, keepdims=True)
        var = jnp.mean(centred * centred, axis=1, keepdims=True)
        deviation = lax.rsqrt(var + EPSILON)
        normal = centred * deviation
        scaled = n_ref[r * frames : (r + 1) * frames, :] * gain_ref[...]
        residual = deviation * (
            scaled
            - jnp.mean(scaled, axis=1, keepdims=True)
            - normal * jnp.mean(scaled * normal, axis=1, keepdims=True)
        )
        out_ref[r] = (g_ref[r].astype(F32) + residual).astype(BF16)


def finish(owners, pieces, back, inputs, grads, gain):
    records, frames, width = inputs.shape
    anywhere = pl.BlockSpec(memory_space=pltpu.HBM)
    depth = pieces[0].shape[1]
    return pl.pallas_call(
        finish_kernel,
        grid=(1,),
        out_shape=jax.ShapeDtypeStruct(inputs.shape, BF16),
        in_specs=[pl.BlockSpec(memory_space=pltpu.SMEM)]
        + [fixed(array) for array in (back, inputs, grads, gain)]
        + [anywhere] * len(pieces),
        out_specs=fixed(inputs),
        scratch_shapes=[
            pltpu.VMEM((records * frames, depth), BF16),
            pltpu.VMEM((records * frames, width), F32),
            pltpu.VMEM((width, depth), BF16),
            pltpu.SemaphoreType.DMA((len(pieces),)),
        ],
        compiler_params=pltpu.CompilerParams(vmem_limit_bytes=ROOM),
        cost_estimate=cost(2 * records * frames * width * depth, 2 * depth * width),
    )(owners, back, inputs, grads, gain, *pieces)


def exchange(items, groups=None):
    return lax.all_to_all(items, "seq", split_axis=0, concat_axis=0, tiled=True, axis_index_groups=groups)


def after(value, *others):
    return lax.optimization_barrier((value,) + others)[0]


def across(rows, dy, dx):
    return lax.ppermute(rows, "seq", seq_pairs(dy, dx, 0))


STEPS = ((0, 0), (0, 1), (1, 0), (3, 0), (1, 1), (3, 1), (2, 0), (2, 1))


def nearby(group):
    return [across(group, *step) for step in STEPS[1:4]]


def further(near):
    partner, below, _ = near
    return [across(partner, 1, 0), across(partner, 3, 0), across(below, 1, 0)]


def on_device(
    layer_input,
    norm_gain,
    queries,
    key_states,
    value_states,
    out_grad,
    out_weight,
    qkv_weight,
    lengths,
):
    frames, records, features = queries.shape[1:]
    width = out_grad.shape[3]
    seq = lax.axis_index("seq").astype(jnp.int32)
    y, x = seq // (X * Z), lax.rem(seq // Z, X)
    places = jnp.stack([lax.rem(y - dy + Y, Y) * X + lax.rem(x - dx + X, X) for dy, dx in STEPS])
    z_groups = [[g * Z + k for k in range(Z)] for g in range(X * Y)]

    copies = jnp.broadcast_to(out_weight, (Z,) + out_weight.shape[1:])
    out_group = exchange(copies, z_groups).reshape(-1, width)
    flat = lambda array: array[0].reshape(frames, records * features)
    packed = pack_items(flat(queries), flat(key_states))
    packed_values = pack_items(flat(value_states))
    received = exchange(after(packed, out_group))
    near = nearby(out_group)
    received_values = exchange(after(packed_values, received, *near))
    grads = out_grad[0].transpose(1, 0, 2)
    inputs = layer_input[0].transpose(1, 0, 2)
    far = further(near)
    out_pieces = [out_group] + near + far + [across(far[2], 0, 1)]

    record = seq // HEADS
    valid = jnp.sum(jnp.where(jnp.arange(records) == record, lengths[0], 0)).reshape(1)
    keys, queries_t, keys_t = prepare(valid, received)
    weights_0, sums_0 = softmax_weights(0, after(valid, *near), keys, queries_t)
    attn_grad = project(after(places, sums_0), grads.reshape(records * frames, width), out_pieces)
    received_grads = exchange(after(attn_grad, received_values))
    weights_1, sums_1 = softmax_weights(1, after(valid, attn_grad), keys, queries_t)
    copies = jnp.broadcast_to(qkv_weight, (Z,) + qkv_weight.shape[1:])
    qkv_group = exchange(after(copies, received_grads, sums_1), z_groups).reshape(-1, qkv_weight.shape[2])
    rest = (queries_t, keys_t, received_values, received_grads)
    begun = attention_grads(0, weights_0, after(sums_0, sums_1), *rest)
    near = nearby(qkv_group)
    gradients = attention_grads(1, weights_1, after(sums_1, qkv_group), *rest, begun)
    gradients, *near = lax.optimization_barrier((gradients, *near))
    back = exchange(gradients)
    partner, below, above = near
    diagonal = [across(below, 0, 1), across(partner, 3, 0)]
    far = [across(below, 1, 0), across(diagonal[1], 3, 0)]
    result = finish(places, [qkv_group] + near + diagonal + far, back, inputs, grads, norm_gain)
    count = lax.axis_size("section")
    moved = lax.ppermute(result, "section", [(i, (i - 1) % count) for i in range(count)])
    return moved.transpose(1, 0, 2)[None]


def solution(mesh):
    rows = P("section", "seq", None, None)
    in_specs = (
        rows,
        P("section", None),
        rows,
        rows,
        rows,
        rows,
        P("section", "seq", None),
        P("section", "seq", None),
        P("section", None),
    )
    return jax.shard_map(on_device, mesh=mesh, in_specs=in_specs, out_specs=rows, check_vma=False)
```

```python
import functools

import jax
import jax.numpy as jnp
from jax import lax
from jax.experimental import pallas as pl
from jax.experimental.pallas import tpu as pltpu
from jax.sharding import PartitionSpec as P

HEADS = 16
HS = 64
EPSILON = 1e-05
MASKED = -1e30
SCALE = HS**-0.5
ROW_DOT = (((1,), (1,)), ((), ()))
PLAIN_DOT = (((1,), (0,)), ((), ()))
MIB = 1024 * 1024
QB = 256
KB = 256
UNROLL1 = True
UNROLL2 = True
Y, X, Z = 4, 2, 8
BF16 = jnp.bfloat16
F32 = jnp.float32
WHOLE = pl.BlockSpec(memory_space=pltpu.VMEM)
ROOM = 60 * MIB


def cost(flops, moved, exps=0):
    return pl.CostEstimate(flops=flops, bytes_accessed=moved, transcendentals=exps)


def fixed(array):
    return pl.BlockSpec(array.shape, lambda i: (0,) * len(array.shape))


def halves(even, odd):
    first = jnp.concatenate([even[:, :HS], odd[:, :HS]], axis=1)
    second = jnp.concatenate([even[:, HS:], odd[:, HS:]], axis=1)
    return first, second


def seq_pairs(dy, dx, dz):
    pairs = []
    for y in range(Y):
        for x in range(X):
            for z in range(Z):
                to = ((y + dy) % Y) * X * Z + ((x + dx) % X) * Z + (z + dz) % Z
                pairs.append((y * X * Z + x * Z + z, to))
    return pairs


def pack_kernel(*refs):
    out_ref = refs[-1]
    half = refs[0].shape[0] // 2
    for n, ref in enumerate(refs[:-1]):
        for pair in range(ref.shape[1] // 128):
            tile = ref[:, pair * 128 : (pair + 1) * 128]
            first, second = halves(tile[:half], tile[half:])
            out_ref[2 * pair, n * half : (n + 1) * half, :] = first
            out_ref[2 * pair + 1, n * half : (n + 1) * half, :] = second


def pack_items(*arrays):
    frames, lanes = arrays[0].shape
    count = len(arrays)
    return pl.pallas_call(
        pack_kernel,
        out_shape=jax.ShapeDtypeStruct((lanes // HS, count * frames // 2, 128), BF16),
        in_specs=[WHOLE] * count,
        out_specs=WHOLE,
        compiler_params=pltpu.CompilerParams(vmem_limit_bytes=16 * MIB),
        cost_estimate=cost(0, count * MIB),
    )(*arrays)


def project_kernel(owner_ref, grad_ref, *refs):
    out_ref = refs[-1]
    records = grad_ref.shape[0] // 64
    grads = grad_ref[...]
    for n, ref in enumerate(refs[:-1]):
        owner = owner_ref[n]
        tile = lax.dot_general(grads, ref[...], ROW_DOT, preferred_element_type=F32).astype(BF16)
        for r in range(records):
            first, second = halves(tile[r * 64 : r * 64 + 32], tile[r * 64 + 32 : r * 64 + 64])
            out_ref[r * HEADS + 2 * owner] = first
            out_ref[r * HEADS + 2 * owner + 1] = second


def project(owners, grads, pieces):
    rows, width = grads.shape
    items = (rows // 64) * HEADS
    return pl.pallas_call(
        project_kernel,
        out_shape=jax.ShapeDtypeStruct((items, 32, 128), BF16),
        in_specs=[pl.BlockSpec(memory_space=pltpu.SMEM)] + [WHOLE] * (1 + len(pieces)),
        out_specs=WHOLE,
        compiler_params=pltpu.CompilerParams(vmem_limit_bytes=20 * MIB),
        cost_estimate=cost(2 * rows * width * 1024, 2 * (rows * width + 1024 * width + rows * 1024)),
    )(owners, grads, *pieces)


def fold(values, op):
    return op(values.reshape(values.shape[0] // 8, 8, values.shape[1]), axis=0)


def prepare_kernel(length_ref, r_ref, kz_ref, qt_ref, kt_ref):
    sources = r_ref.shape[0]
    rows = sources * 32
    length = 2 * rows
    valid = length_ref[0]
    packed_q = r_ref[:, 0:32, :].reshape(rows, 128)
    packed_k = r_ref[:, 32:64, :].reshape(rows, 128)
    q_turned = packed_q.T
    k_turned = packed_k.T
    for half in range(2):
        qt_ref[0:HS, half * rows : (half + 1) * rows] = q_turned[half * HS : (half + 1) * HS, :]
        kt_ref[:, half * rows : (half + 1) * rows] = k_turned[half * HS : (half + 1) * HS, :]
    row_id = lax.broadcasted_iota(jnp.int32, (HS, length), 0)
    qt_ref[HS:128, :] = jnp.where(row_id == 0, 1.0, 0.0).astype(BF16)
    spot = lax.broadcasted_iota(jnp.int32, (rows, HS), 0)
    lane = lax.broadcasted_iota(jnp.int32, (rows, HS), 1)
    for half in range(2):
        frame = (spot // 32) * 64 + half * 32 + spot % 32
        bias = jnp.where((lane == 0) & (frame >= valid), MASKED, 0.0).astype(BF16)
        keys = packed_k[:, half * HS : (half + 1) * HS] * SCALE
        kz_ref[half * rows : (half + 1) * rows, :] = jnp.concatenate([keys.astype(BF16), bias], axis=1)


def prepare(valid, received):
    length = received.shape[0] * 64
    out_shape = [
        jax.ShapeDtypeStruct((length, 128), BF16),
        jax.ShapeDtypeStruct((128, length), BF16),
        jax.ShapeDtypeStruct((HS, length), BF16),
    ]
    return pl.pallas_call(
        prepare_kernel,
        grid=(1,),
        out_shape=out_shape,
        in_specs=[pl.BlockSpec(memory_space=pltpu.SMEM), fixed(received)],
        out_specs=[fixed(shape) for shape in out_shape],
        compiler_params=pltpu.CompilerParams(vmem_limit_bytes=ROOM),
        cost_estimate=cost(0, 4 * MIB),
    )(valid, received)


def weights_kernel(gate_ref, kz_ref, qt_ref, w_ref, l_ref, s_ref):
    length = kz_ref.shape[0]
    queries = qt_ref[...]

    def first(j, top):
        at = pl.ds(pl.multiple_of(j * KB, KB), KB)
        s = lax.dot_general(kz_ref[at, :], queries, PLAIN_DOT, preferred_element_type=F32)
        s_ref[at, :] = s
        return jnp.maximum(top, fold(s, jnp.max))

    top = lax.fori_loop(0, length // KB, first, jnp.full((8, QB), -jnp.inf, F32), unroll=UNROLL1)
    top = jnp.max(top, axis=0, keepdims=True)

    def second(j, total):
        at = pl.ds(pl.multiple_of(j * KB, KB), KB)
        w = jnp.exp(s_ref[at, :] - top)
        w_ref[0, at, :] = w
        return total + fold(w, jnp.sum)

    total = lax.fori_loop(0, length // KB, second, jnp.zeros((8, QB), F32), unroll=UNROLL1)
    l_ref[...] = jnp.sum(total, axis=0, keepdims=True)


def softmax_weights(part, gate, keys, queries_t):
    length = keys.shape[0]
    blocks = length // QB // 2
    return pl.pallas_call(
        weights_kernel,
        grid=(blocks,),
        out_shape=[
            jax.ShapeDtypeStruct((blocks, length, QB), F32),
            jax.ShapeDtypeStruct((1, length // 2), F32),
        ],
        in_specs=[
            pl.BlockSpec(memory_space=pltpu.SMEM),
            fixed(keys),
            pl.BlockSpec((128, QB), lambda i: (0, part * blocks + i)),
        ],
        out_specs=[
            pl.BlockSpec((1, length, QB), lambda i: (i, 0, 0)),
            pl.BlockSpec((1, QB), lambda i: (0, i)),
        ],
        scratch_shapes=[pltpu.VMEM((length, QB), F32)],
        compiler_params=pltpu.CompilerParams(vmem_limit_bytes=ROOM),
        cost_estimate=cost(4 * length * length * HS, 2 * length * length, length * length // 2),
    )(gate, keys, queries_t)


def grads_kernel(part, w_ref, l_ref, qt_ref, kt_ref, r_ref, g_ref, *refs):
    if part == 0:
        dq_ref, acc_ref, gt_ref, dp_ref = refs
    else:
        begun_dq_ref, begun_ref, out_ref, gt_ref, dp_ref, acc_ref, dq_ref = refs
    step = pl.program_id(0)
    sources = r_ref.shape[0]
    rows = sources * 32
    length = 2 * rows
    per = KB // 32

    @pl.when(step == 0)
    def _():
        gt_ref[...] = g_ref[...].reshape(rows, 128).T[part * HS : (part + 1) * HS, :]
        acc_ref[...] = jnp.zeros_like(acc_ref) if part == 0 else begun_ref[...]

    here = pl.ds(pl.multiple_of(step * QB, QB), QB)
    grads = gt_ref[:, here]
    none = jnp.zeros((HS, QB), BF16)
    inverse = 1.0 / l_ref[...]

    def first(half, side, j, centre):
        at = pl.ds(pl.multiple_of(half * rows + j * KB, KB), KB)
        values = r_ref[pl.ds(j * per, per), 64:96, :].reshape(KB, 128)
        dp = lax.dot_general(values, side, PLAIN_DOT, preferred_element_type=F32)
        dp_ref[at, :] = dp
        return centre + fold(w_ref[0, at, :] * inverse * dp, jnp.sum)

    centre = jnp.zeros((8, QB), F32)
    for half in range(2):
        side = jnp.concatenate([grads, none] if half == 0 else [none, grads], axis=0)
        centre = lax.fori_loop(0, rows // KB, functools.partial(first, half, side), centre, unroll=UNROLL2)
    centre = jnp.sum(centre, axis=0, keepdims=True)

    scaled_q = (qt_ref[0:HS, :] * SCALE).astype(BF16)
    side_t = jnp.concatenate([scaled_q, none], axis=0)
    side_w = jnp.concatenate([none, grads], axis=0)

    def second(j, dqt):
        at = pl.ds(pl.multiple_of(j * KB, KB), KB)
        p = w_ref[0, at, :] * inverse
        t = (p * (dp_ref[at, :] - centre)).astype(BF16)
        acc_ref[at, :] += lax.dot_general(
            t, side_t, ROW_DOT, preferred_element_type=F32
        ) + lax.dot_general(p.astype(BF16), side_w, ROW_DOT, preferred_element_type=F32)
        return dqt + lax.dot_general(kt_ref[:, at], t, PLAIN_DOT, preferred_element_type=F32)

    dqt = lax.fori_loop(0, length // KB, second, jnp.zeros((HS, QB), F32), unroll=UNROLL2)
    dq_ref[:, here] = dqt * SCALE

    if part == 1:

        @pl.when(step == pl.num_programs(0) - 1)
        def _():
            both = jnp.concatenate([begun_dq_ref[...], dq_ref[...]], axis=0)
            out_ref[:, 0:32, :] = both.T.astype(BF16).reshape(sources, 32, 128)
            for half in range(2):
                lanes = acc_ref[half * rows : (half + 1) * rows, :].astype(BF16)
                at = slice(32 + half * 32, 64 + half * 32)
                out_ref[:, at, :] = lanes.reshape(sources, 32, 128)


def attention_grads(part, weights, sums, queries_t, keys_t, received, received_grads, begun=()):
    blocks, length, _ = weights.shape
    sources = received.shape[0]
    dq = jax.ShapeDtypeStruct((HS, length // 2), F32)
    acc = jax.ShapeDtypeStruct((length, 128), F32)
    scratch = [pltpu.VMEM((HS, length // 2), BF16), pltpu.VMEM((length, QB), F32)]
    if part == 0:
        out_shape = [dq, acc]
    else:
        out_shape = jax.ShapeDtypeStruct((sources, 96, 128), BF16)
        scratch += [pltpu.VMEM((length, 128), F32), pltpu.VMEM((HS, length // 2), F32)]
    return pl.pallas_call(
        functools.partial(grads_kernel, part),
        grid=(blocks,),
        out_shape=out_shape,
        in_specs=[
            pl.BlockSpec((1, length, QB), lambda i: (i, 0, 0)),
            pl.BlockSpec((1, QB), lambda i: (0, i)),
            pl.BlockSpec((128, QB), lambda i: (0, part * blocks + i)),
        ]
        + [fixed(array) for array in (keys_t, received, received_grads, *begun)],
        out_specs=jax.tree.map(fixed, out_shape),
        scratch_shapes=scratch,
        compiler_params=pltpu.CompilerParams(vmem_limit_bytes=ROOM),
        cost_estimate=cost(16 * length * length * HS, 2 * length * length),
    )(weights, sums, queries_t, keys_t, received, received_grads, *begun)


def finish_kernel(owner_ref, back_ref, x_ref, g_ref, gain_ref, *refs):
    pieces, (out_ref, j_ref, n_ref, w_ref, sems) = refs[:-5], refs[-5:]
    copies = []
    for n, piece in enumerate(pieces):
        rows = piece.shape[0]
        to = pl.ds(pl.multiple_of(owner_ref[n] * rows, rows), rows)
        copies.append(pltpu.make_async_copy(piece, w_ref.at[to, :], sems.at[n]))
        copies[-1].start()
    records = x_ref.shape[0]
    frames = x_ref.shape[1]
    width = x_ref.shape[2]
    features = HEADS * HS
    for r in range(records):
        for pair in range(HEADS // 2):
            item = r * HEADS + 2 * pair
            at = slice(pair * 128, (pair + 1) * 128)
            first, second = halves(back_ref[item, 0:32], back_ref[item + 1, 0:32])
            j_ref[r * frames : r * frames + 32, at] = first
            j_ref[r * frames + 32 : (r + 1) * frames, at] = second
            keys, values = halves(back_ref[item, 32:96], back_ref[item + 1, 32:96])
            span = slice(r * frames, (r + 1) * frames)
            j_ref[span, features + pair * 128 : features + (pair + 1) * 128] = keys
            j_ref[span, 2 * features + pair * 128 : 2 * features + (pair + 1) * 128] = values
    for copy in copies:
        copy.wait()
    step = 256
    for n in range(width // step):
        n_ref[:, n * step : (n + 1) * step] = lax.dot_general(
            j_ref[...], w_ref[n * step : (n + 1) * step, :], ROW_DOT, preferred_element_type=F32
        )
    for r in range(records):
        x = x_ref[r].astype(F32)
        centred = x - jnp.mean(x, axis=1, keepdims=True)
        var = jnp.mean(centred * centred, axis=1, keepdims=True)
        deviation = lax.rsqrt(var + EPSILON)
        normal = centred * deviation
        scaled = n_ref[r * frames : (r + 1) * frames, :] * gain_ref[...]
        residual = deviation * (
            scaled
            - jnp.mean(scaled, axis=1, keepdims=True)
            - normal * jnp.mean(scaled * normal, axis=1, keepdims=True)
        )
        out_ref[r] = (g_ref[r].astype(F32) + residual).astype(BF16)


def finish(owners, pieces, back, inputs, grads, gain):
    records, frames, width = inputs.shape
    anywhere = pl.BlockSpec(memory_space=pltpu.HBM)
    depth = pieces[0].shape[1]
    return pl.pallas_call(
        finish_kernel,
        grid=(1,),
        out_shape=jax.ShapeDtypeStruct(inputs.shape, BF16),
        in_specs=[pl.BlockSpec(memory_space=pltpu.SMEM)]
        + [fixed(array) for array in (back, inputs, grads, gain)]
        + [anywhere] * len(pieces),
        out_specs=fixed(inputs),
        scratch_shapes=[
            pltpu.VMEM((records * frames, depth), BF16),
            pltpu.VMEM((records * frames, width), F32),
            pltpu.VMEM((width, depth), BF16),
            pltpu.SemaphoreType.DMA((len(pieces),)),
        ],
        compiler_params=pltpu.CompilerParams(vmem_limit_bytes=ROOM),
        cost_estimate=cost(2 * records * frames * width * depth, 2 * depth * width),
    )(owners, back, inputs, grads, gain, *pieces)


def exchange(items, groups=None):
    return lax.all_to_all(items, "seq", split_axis=0, concat_axis=0, tiled=True, axis_index_groups=groups)


def after(value, *others):
    return lax.optimization_barrier((value,) + others)[0]


def across(rows, dy, dx):
    return lax.ppermute(rows, "seq", seq_pairs(dy, dx, 0))


STEPS = ((0, 0), (0, 1), (1, 0), (3, 0), (1, 1), (3, 1), (2, 0), (2, 1))


def nearby(group):
    return [across(group, *step) for step in STEPS[1:4]]


def further(near):
    partner, below, _ = near
    return [across(partner, 1, 0), across(partner, 3, 0), across(below, 1, 0)]


def on_device(
    layer_input,
    norm_gain,
    queries,
    key_states,
    value_states,
    out_grad,
    out_weight,
    qkv_weight,
    lengths,
):
    frames, records, features = queries.shape[1:]
    width = out_grad.shape[3]
    seq = lax.axis_index("seq").astype(jnp.int32)
    y, x = seq // (X * Z), lax.rem(seq // Z, X)
    places = jnp.stack([lax.rem(y - dy + Y, Y) * X + lax.rem(x - dx + X, X) for dy, dx in STEPS])
    z_groups = [[g * Z + k for k in range(Z)] for g in range(X * Y)]

    copies = jnp.broadcast_to(out_weight, (Z,) + out_weight.shape[1:])
    out_group = exchange(copies, z_groups).reshape(-1, width)
    flat = lambda array: array[0].reshape(frames, records * features)
    packed = pack_items(flat(queries), flat(key_states), flat(value_states))
    received = exchange(after(packed, out_group))
    near = nearby(out_group)
    grads = out_grad[0].transpose(1, 0, 2)
    inputs = layer_input[0].transpose(1, 0, 2)
    far = further(near)
    out_pieces = [out_group] + near + far + [across(far[2], 0, 1)]

    record = seq // HEADS
    valid = jnp.sum(jnp.where(jnp.arange(records) == record, lengths[0], 0)).reshape(1)
    keys, queries_t, keys_t = prepare(valid, received)
    copies = jnp.broadcast_to(qkv_weight, (Z,) + qkv_weight.shape[1:])
    qkv_group = exchange(after(copies, far[2], *near), z_groups).reshape(-1, qkv_weight.shape[2])
    weights_0, sums_0 = softmax_weights(0, after(valid, *near), keys, queries_t)
    attn_grad = project(after(places, sums_0), grads.reshape(records * frames, width), out_pieces)
    received_grads = exchange(after(attn_grad, qkv_group))
    weights_1, sums_1 = softmax_weights(1, after(valid, attn_grad), keys, queries_t)
    rest = (queries_t, keys_t, received, received_grads)
    begun = attention_grads(0, weights_0, after(sums_0, sums_1), *rest)
    near = nearby(after(qkv_group, attn_grad))
    sums_1, *near = lax.optimization_barrier((sums_1, *near))
    gradients = attention_grads(1, weights_1, sums_1, *rest, begun)
    partner, below, above = near
    diagonal = [across(partner, 1, 0), across(partner, 3, 0)]
    gradients, *diagonal = lax.optimization_barrier((gradients, *diagonal))
    back = exchange(gradients)
    far = [across(after(below, gradients), 1, 0), across(diagonal[1], 3, 0)]
    result = finish(places, [qkv_group] + near + diagonal + far, back, inputs, grads, norm_gain)
    count = lax.axis_size("section")
    moved = lax.ppermute(result, "section", [(i, (i - 1) % count) for i in range(count)])
    return moved.transpose(1, 0, 2)[None]


def solution(mesh):
    rows = P("section", "seq", None, None)
    in_specs = (
        rows,
        P("section", None),
        rows,
        rows,
        rows,
        rows,
        P("section", "seq", None),
        P("section", "seq", None),
        P("section", None),
    )
    return jax.shard_map(on_device, mesh=mesh, in_specs=in_specs, out_specs=rows, check_vma=False)
```
